256 devices in a mesh: seq: 8 (over z), fsdp: 32 (over y, x, core).
Axes of the slice: x: 4, y: 4, z: 8, core: 2. Of those that a mesh axis runs over, the one named last changes fastest.
Arguments:
- tokens: bfloat16 [4096, 4096], P('seq', 'fsdp'), may hold values from -6 to 6
- in_mask: int32 [4096, 4096], P('seq', 'fsdp'), may hold values 0 or 1
- out_mask: int32 [4096, 32, 384], P('seq', 'fsdp'), may hold values 0 or 1
- w_mean: bfloat16 [4096, 32, 384], P('seq', 'fsdp'), may hold values from -0.09375 to 0.09375
- w_sigma: bfloat16 [4096, 32, 384], P('seq', 'fsdp'), may hold values from -0.046875 to 0.046875
- grad_out: bfloat16 [4096, 4096], P('seq', 'fsdp'), may hold values from -6 to 6
Outputs:
- attended: bfloat16 [4096, 4096], P('seq', 'fsdp')
- d_tokens: bfloat16 [4096, 4096], P('seq', 'fsdp')
- g_mean: bfloat16 [4096, 32, 384], P('seq', 'fsdp')
- g_sigma: bfloat16 [4096, 32, 384], P('seq', 'fsdp')
The draws below stay inside these ranges and needn't reach their ends.
Inputs may be any that keep to these rules, and one draw needn't show every extreme that they name: `in_mask`: each entry is a sign bit: the sign is 2 * entry - 1. `out_mask`: each entry is a sign bit: the sign is 2 * entry - 1.
All inputs are finite; a program needn't handle non-finite values. No bound on the sum of `in_mask` or of `out_mask` on one device may be relied on, other than what follows from the above.
Results may differ from the reference program's by a relative error of at most 0.017.
Values may be sent and summed in bfloat16 or wider, within the bound.
A program may use at most 64 MiB of HBM per device.

```python
import jax
import jax.numpy as jnp
from jax import lax

D = 4096
E = 128
HEADS_DEV = 1
TOK_DEV = 512
H = 32
S = 4096
N_SEQ = 8
N_FSDP = 32


def place_ends(drawn, key, least, largest):
    dims = drawn.shape
    spot = [jax.random.randint(jax.random.fold_in(key, axis), (), 0, dims[axis]) for axis in range(len(dims))]
    drawn = drawn.at[tuple(spot)].set(least)
    longest = dims.index(max(dims))
    spot[longest] = (spot[longest] + 1) % dims[longest]
    return drawn.at[tuple(spot)].set(largest)


def shard_levels(stream_key, dims, pieces, least, high):
    def one(dim, shards_of):
        draws = jax.random.uniform(jax.random.fold_in(jax.random.fold_in(stream_key, 6), dim), (shards_of,), jnp.float32, least / len(pieces), high / len(pieces))
        return jnp.repeat(jnp.exp(draws), dims[dim] // shards_of).reshape((-1,) + (1,) * (len(dims) - dim - 1))

    level = one(*pieces[0])
    for cut in pieces[1:]:
        level = level * one(*cut)
    return level


def gaussian(key, shape, deviation, most, shards=(), dtype=jnp.bfloat16):
    array = deviation * jax.random.normal(key, shape, jnp.float32)
    if shards:
        array = array * shard_levels(key, shape, shards, -0.22, 0.18)
    return jnp.clip(array, -most, most).astype(dtype)


def setup_inputs(seed: int = 0) -> dict:
    keys = jax.random.split(jax.random.key(seed), 7)
    tokens = gaussian(keys[0], (S, D), 1.0, 6.0, ((0, 8), (1, 32)))
    in_mask = place_ends((jax.random.randint(keys[1], (S, D), 0, 2) < 1).astype(jnp.int32), jax.random.fold_in(keys[1], 1), 0, 1)
    out_mask = place_ends((jax.random.randint(keys[2], (S, H, 3 * E), 0, 2) < 1).astype(jnp.int32), jax.random.fold_in(keys[2], 1), 0, 1)
    w_mean = gaussian(keys[3], (D, H, 3 * E), D ** -0.5, 0.09375, ((0, 8), (1, 32)))
    w_sigma = gaussian(keys[4], (D, H, 3 * E), (4 * D) ** -0.5, 0.046875, ((0, 8), (1, 32)))
    grad_out = gaussian(keys[5], (S, H * E), 1.0, 6.0, ((0, 8), (1, 32)))
    return {"tokens": tokens, "in_mask": in_mask, "out_mask": out_mask, "w_mean": w_mean, "w_sigma": w_sigma, "grad_out": grad_out}


EPSILON = 1e-06

def feature_map(u):
    return jnp.where(u > 0, u + 1.0, jnp.exp(jnp.minimum(u, 0.0)))

def feature_slope(u):
    return jnp.where(u > 0, 1.0, jnp.exp(jnp.minimum(u, 0.0)))

def head_pass(pair):
    highest = lax.Precision.HIGHEST
    projected_head, upstream_head = pair
    seq_len = projected_head.shape[0]
    blocks = seq_len // TOK_DEV
    pre_query = projected_head[:, :E]
    pre_keys = projected_head[:, E:2 * E]
    queries = feature_map(pre_query)
    key_feats = feature_map(pre_keys)
    values = projected_head[:, 2 * E:]
    causal = (lax.broadcasted_iota(jnp.int32, (TOK_DEV, TOK_DEV), 0) >= lax.broadcasted_iota(jnp.int32, (TOK_DEV, TOK_DEV), 1)).astype(jnp.float32)
    q_blocks = queries.reshape(blocks, TOK_DEV, E)
    k_blocks = key_feats.reshape(blocks, TOK_DEV, E)
    v_blocks = values.reshape(blocks, TOK_DEV, E)

    def forward_step(state, block):
        q_blk, k_blk, v_blk = block
        scores = jnp.dot(q_blk, k_blk.T, precision=highest) * causal
        numer = jnp.dot(scores, v_blk, precision=highest) + jnp.dot(q_blk, state, precision=highest)
        return (state + jnp.dot(k_blk.T, v_blk, precision=highest), (numer, state))
    start_state = jnp.zeros((E, E), jnp.float32)
    last_state, (numerator, incoming) = lax.scan(forward_step, start_state, (q_blocks, k_blocks, v_blocks))
    numerator = numerator.reshape(seq_len, E)
    inv_norm = lax.rsqrt(lax.optimization_barrier(jnp.mean(numerator * numerator, axis=-1, keepdims=True)) + EPSILON)
    normed = numerator * inv_norm
    d_numer = inv_norm * (upstream_head - normed * lax.optimization_barrier(jnp.mean(upstream_head * normed, axis=-1, keepdims=True)))
    dn_blocks = d_numer.reshape(blocks, TOK_DEV, E)

    def backward_step(suffix, block):
        q_blk, k_blk, v_blk, dn_blk, state_in = block
        scores = jnp.dot(q_blk, k_blk.T, precision=highest) * causal
        d_scores = jnp.dot(dn_blk, v_blk.T, precision=highest) * causal
        d_query = jnp.dot(d_scores, k_blk, precision=highest) + jnp.dot(dn_blk, state_in.T, precision=highest)
        d_keys = jnp.dot(d_scores.T, q_blk, precision=highest) + jnp.dot(v_blk, suffix.T, precision=highest)
        d_values = jnp.dot(scores.T, dn_blk, precision=highest) + jnp.dot(k_blk, suffix, precision=highest)
        return (suffix + jnp.dot(q_blk.T, dn_blk, precision=highest), (d_query, d_keys, d_values))
    last_suffix, (d_query, d_keys, d_values) = lax.scan(backward_step, start_state, (q_blocks, k_blocks, v_blocks, dn_blocks, incoming), reverse=True)
    d_query = d_query.reshape(seq_len, E) * feature_slope(pre_query)
    d_keys = d_keys.reshape(seq_len, E) * feature_slope(pre_keys)
    d_values = d_values.reshape(seq_len, E)
    return (normed, jnp.concatenate([d_query, d_keys, d_values], axis=-1))

def reference(tokens, in_mask, out_mask, w_mean, w_sigma, grad_out):
    seq_len = tokens.shape[0]
    columns = H * 3 * E
    in_sign = (2 * in_mask - 1).astype(jnp.bfloat16)
    flipped = tokens * in_sign
    out_sign = (2 * out_mask - 1).astype(jnp.float32)
    projected = jnp.dot(tokens, w_mean.reshape(D, columns), preferred_element_type=jnp.float32)
    projected = projected + jnp.dot(flipped, w_sigma.reshape(D, columns), preferred_element_type=jnp.float32) * out_sign.reshape(seq_len, columns)
    projected = jnp.transpose(projected.reshape(seq_len, H, 3 * E), (1, 0, 2))
    upstream = jnp.transpose(grad_out.astype(jnp.float32).reshape(seq_len, H, E), (1, 0, 2))
    normed, grad_pre = lax.map(head_pass, (projected, upstream))
    attended = jnp.transpose(normed, (1, 0, 2)).reshape(seq_len, H * E).astype(jnp.bfloat16)
    grad_mean = jnp.transpose(grad_pre, (1, 0, 2)).astype(jnp.bfloat16)
    grad_sigma = grad_mean * out_sign.astype(jnp.bfloat16)
    gm_flat = grad_mean.reshape(seq_len, columns)
    gs_flat = grad_sigma.reshape(seq_len, columns)

    def weight_step(running, block):
        tok_block, flip_block, gm_block, gs_block = block
        part_mean = jnp.dot(tok_block.T, gm_block, preferred_element_type=jnp.float32)
        part_sigma = jnp.dot(flip_block.T, gs_block, preferred_element_type=jnp.float32)
        part_mean = lax.optimization_barrier(part_mean.astype(jnp.bfloat16)).astype(jnp.float32)
        part_sigma = lax.optimization_barrier(part_sigma.astype(jnp.bfloat16)).astype(jnp.float32)
        return ((running[0] + part_mean, running[1] + part_sigma), None)
    zero_weights = jnp.zeros((D, columns), jnp.float32)
    (sum_mean, sum_sigma), unused = lax.scan(weight_step, (zero_weights, zero_weights), (tokens.reshape(N_SEQ, TOK_DEV, D), flipped.reshape(N_SEQ, TOK_DEV, D), gm_flat.reshape(N_SEQ, TOK_DEV, columns), gs_flat.reshape(N_SEQ, TOK_DEV, columns)))
    group_cols = HEADS_DEV * 3 * E
    gm_groups = jnp.transpose(gm_flat.reshape(seq_len, N_FSDP, group_cols), (1, 0, 2))
    gs_groups = jnp.transpose(gs_flat.reshape(seq_len, N_FSDP, group_cols), (1, 0, 2))
    wm_groups = jnp.transpose(w_mean.reshape(D, N_FSDP, group_cols), (1, 0, 2))
    ws_groups = jnp.transpose(w_sigma.reshape(D, N_FSDP, group_cols), (1, 0, 2))

    def input_step(running, group):
        gm_group, gs_group, wm_group, ws_group = group
        term_mean = jnp.dot(gm_group, wm_group.T, preferred_element_type=jnp.float32)
        term_sigma = jnp.dot(gs_group, ws_group.T, preferred_element_type=jnp.float32)
        term_mean = lax.optimization_barrier(term_mean.astype(jnp.bfloat16)).astype(jnp.float32)
        term_sigma = lax.optimization_barrier(term_sigma.astype(jnp.bfloat16)).astype(jnp.float32)
        return ((running[0] + term_mean, running[1] + term_sigma), None)
    zero_inputs = jnp.zeros((seq_len, D), jnp.float32)
    (back_mean, back_sigma), unused_two = lax.scan(input_step, (zero_inputs, zero_inputs), (gm_groups, gs_groups, wm_groups, ws_groups))
    d_tokens = (back_mean + in_sign.astype(jnp.float32) * back_sigma).astype(jnp.bfloat16)
    g_mean = sum_mean.reshape(D, H, 3 * E).astype(jnp.bfloat16)
    g_sigma = sum_sigma.reshape(D, H, 3 * E).astype(jnp.bfloat16)
    return (attended, d_tokens, g_mean, g_sigma)
```

```python
import jax
import jax.numpy as jnp
from jax import lax
from jax.experimental import pallas as pl
from jax.experimental.pallas import tpu as pltpu
from jax.sharding import PartitionSpec as P

EPSILON = 1e-06
MESH = pl.DeviceIdType.MESH
F32 = jnp.float32
BF16 = jnp.bfloat16
TB = 512
DB = 128
KB = 512
E = 128
C = 3 * E
NZ = 8
HALF = TB // 2


def nn(a, b):
    return lax.dot_general(a, b, (((1,), (0,)), ((), ())), preferred_element_type=F32)


def nt(a, b):
    return lax.dot_general(a, b, (((1,), (1,)), ((), ())), preferred_element_type=F32)


def kernel(
    tok, in_mask, sgn, w_mean, w_sigma, gout,
    att_out, dtok_out, gm_out, gs_out,
    ta, sa, w_all, pm, ps, sts, str_, sus, sur, inc, suf, sc, sct, ds, dst, nu, dki, dvi,
    gb, gsb, gt, gst, gp, rr, bp, cr, xr, yr, xb, yb, xr2, yr2,
    zs, zr, ts, tr, ss, sr, cs, crs, st_s, st_r, su_s, su_r, rs_s, rs_r, bc_s, bc_r, bx_s, bx_r, by_s, by_r,
):
    s = lax.axis_index("seq")
    f = lax.axis_index("fsdp")
    c = lax.rem(f, 2)
    x = lax.rem(lax.div(f, 2), 4)
    y = lax.div(f, 8)
    oc = 1 - c

    def at_seq(k):
        return (lax.rem(s + k, NZ), f)

    def at_x(k):
        return (s, (y * 4 + lax.rem(x + k, 4)) * 2 + c)

    def at_y(k):
        return (s, (lax.rem(y + k, 4) * 4 + x) * 2 + c)

    partner = (s, (y * 4 + x) * 2 + oc)
    pending = []

    def copy(src, dst, send, recv, dev):
        return pltpu.make_async_remote_copy(
            src_ref=src, dst_ref=dst, send_sem=send, recv_sem=recv, device_id=dev, device_id_type=MESH
        )

    def start(src, dst, send, recv, dev):
        one = copy(src, dst, send, recv, dev)
        one.start()
        pending.append(one)

    def arrived(ref, send, recv):
        copy(ref, ref, send, recv, partner).wait_recv()

    barrier = pltpu.get_barrier_semaphore()
    peers = [at_seq(k) for k in range(1, NZ)] + [at_x(k) for k in (1, 2, 3)] + [at_y(k) for k in (1, 2, 3)] + [partner]
    for peer in peers:
        pl.semaphore_signal(barrier, inc=1, device_id=peer, device_id_type=MESH)

    ta[c, y, x] = tok[...]
    sa[c, y, x] = (2 * in_mask[...] - 1).astype(F32).astype(BF16)
    w_all[s, 0] = w_mean[...]
    w_all[s, 1] = w_sigma[...]
    pl.semaphore_wait(barrier, len(peers))

    def ring_out(way, hop, m):
        owner = lax.rem(s + (NZ - hop if way == 0 else hop), NZ)
        ref = w_all.at[owner, m]
        start(ref, ref, zs.at[way, hop, m], zr.at[way, hop, m], at_seq(1 if way == 0 else NZ - 1))

    def ring_in(way, hop, m):
        owner = lax.rem(s + (NZ - 1 - hop if way == 0 else 1 + hop), NZ)
        arrived(w_all.at[owner, m], zs.at[way, hop, m], zr.at[way, hop, m])

    def ring_step(hop, part):
        for way in (0, 1):
            m = part if way == 0 else 1 - part
            ring_in(way, hop, m)
            if hop < 2 or (hop == 2 and part == 0):
                ring_out(way, hop + 1, m)

    for part in (0, 1):
        ring_out(0, 0, part)
        ring_out(1, 0, 1 - part)

    for k in (1, 2, 3):
        start(ta.at[c, y, x], ta.at[c, y, x], ts.at[k - 1], tr.at[k - 1], at_x(k))
        start(sa.at[c, y, x], sa.at[c, y, x], ss.at[k - 1], sr.at[k - 1], at_y(k))
    for k in (1, 2, 3):
        arrived(ta.at[c, y, lax.rem(x + 4 - k, 4)], ts.at[k - 1], tr.at[k - 1])
    for k in (1, 2, 3):
        start(ta.at[c, y], ta.at[c, y], ts.at[2 + k], tr.at[2 + k], at_y(k))
    for k in (1, 2, 3):
        arrived(sa.at[c, lax.rem(y + 4 - k, 4), x], ss.at[k - 1], sr.at[k - 1])
    for k in (1, 2, 3):
        start(sa.at[c, :, x], sa.at[c, :, x], ss.at[2 + k], sr.at[2 + k], at_x(k))
    start(ta.at[c, y], ta.at[c, y], cs.at[0], crs.at[0], partner)
    start(sa.at[c, :, x], sa.at[c, :, x], cs.at[4], crs.at[4], partner)

    ring_step(0, 0)
    ring_step(0, 1)
    ring_step(1, 0)
    for k in (1, 2, 3):
        yk = lax.rem(y + 4 - k, 4)
        arrived(ta.at[c, yk], ts.at[2 + k], tr.at[2 + k])
        start(ta.at[c, yk], ta.at[c, yk], cs.at[k], crs.at[k], partner)
        xk = lax.rem(x + 4 - k, 4)
        arrived(sa.at[c, :, xk], ss.at[2 + k], sr.at[2 + k])
        start(sa.at[c, :, xk], sa.at[c, :, xk], cs.at[4 + k], crs.at[4 + k], partner)
    ring_step(1, 1)
    for k in range(4):
        arrived(ta.at[oc, lax.rem(y + 4 - k, 4)], cs.at[k], crs.at[k])
        arrived(sa.at[oc, :, lax.rem(x + 4 - k, 4)], cs.at[4 + k], crs.at[4 + k])

    def columns(ref, e):
        row, first = lax.div(e, 2), 2 * lax.rem(e, 2)
        return jnp.concatenate([ref[j % 2, row, first + j // 2] for j in range(4)], axis=1)

    pm[...] = jnp.zeros_like(pm)
    ps[...] = jnp.zeros_like(ps)

    def project(first, stride, count):
        def one(i, carry):
            owner = lax.rem(s + first + i * stride, NZ)
            t = columns(ta, owner)
            pm[...] += nn(t, w_all[owner, 0])
            ps[...] += nn(t * columns(sa, owner), w_all[owner, 1])
            return carry

        lax.fori_loop(0, count, one, 0)

    project(NZ - 2, 1, 5)
    ring_step(2, 0)
    ring_step(2, 1)
    project(NZ - 3, 6, 2)
    ring_in(0, 3, 0)
    ring_in(1, 3, 1)
    project(4, 1, 1)

    so = sgn[...].astype(F32)
    pre = pm[...] + ps[...] * so
    uq, uk, v = pre[:, :E], pre[:, E : 2 * E], pre[:, 2 * E :]
    exp_q, exp_k = jnp.exp(jnp.minimum(uq, 0.0)), jnp.exp(jnp.minimum(uk, 0.0))
    q = jnp.where(uq > 0, uq + 1.0, exp_q)
    kf = jnp.where(uk > 0, uk + 1.0, exp_k)
    slope_q = jnp.where(uq > 0, 1.0, exp_q)
    slope_k = jnp.where(uk > 0, 1.0, exp_k)
    qb, kb, vb = q.astype(BF16), kf.astype(BF16), v.astype(BF16)

    sts[...] = nn(jnp.transpose(kf).astype(BF16), vb).astype(BF16)
    for k in range(1, NZ):
        @pl.when(s + k < NZ)
        def _():
            copy(sts, str_.at[k - 1], st_s.at[k - 1], st_r.at[k - 1], at_seq(k)).start()

    rows = lax.broadcasted_iota(jnp.int32, (TB, TB), 0)
    cols = lax.broadcasted_iota(jnp.int32, (TB, TB), 1)
    sc[...] = jnp.where(rows >= cols, nt(qb, kb), 0.0).astype(BF16)
    sct[...] = jnp.where(rows <= cols, nt(kb, qb), 0.0).astype(BF16)
    nu[...] = nn(sc[...], vb)
    inc[...] = jnp.zeros_like(inc)
    for k in range(1, NZ):
        @pl.when(s >= k)
        def _():
            arrived(str_.at[k - 1], st_s.at[k - 1], st_r.at[k - 1])
            inc[...] += str_[k - 1].astype(F32)

    inb = inc[...].astype(BF16)
    num = nu[...] + nn(qb, inb)
    inv = lax.rsqrt(jnp.mean(num * num, axis=-1, keepdims=True) + EPSILON)
    normed = num * inv
    att_out[...] = normed.astype(BF16)
    up = gout[...].astype(F32)
    dn = inv * (up - normed * jnp.mean(up * normed, axis=-1, keepdims=True))
    dnb = dn.astype(BF16)
    sus[...] = nn(jnp.transpose(q).astype(BF16), dnb).astype(BF16)
    for k in range(1, NZ):
        @pl.when(s >= k)
        def _():
            copy(sus, sur.at[k - 1], su_s.at[k - 1], su_r.at[k - 1], at_seq(NZ - k)).start()

    ds[...] = jnp.where(rows >= cols, nt(dnb, vb), 0.0).astype(BF16)
    dst[...] = jnp.where(rows <= cols, nt(vb, dnb), 0.0).astype(BF16)
    dq = (nn(ds[...], kb) + nt(dnb, inb)) * slope_q
    dki[...] = nn(dst[...], qb)
    dvi[...] = nn(sct[...], dnb)
    suf[...] = jnp.zeros_like(suf)
    for k in range(1, NZ):
        @pl.when(s + k < NZ)
        def _():
            arrived(sur.at[k - 1], su_s.at[k - 1], su_r.at[k - 1])
            suf[...] += sur[k - 1].astype(F32)

    sfb = suf[...].astype(BF16)
    dk = (dki[...] + nt(vb, sfb)) * slope_k
    dv = dvi[...] + nn(kb, sfb)
    grad = jnp.concatenate([dq, dk, dv], axis=1)
    signed = grad * so
    gb[...] = grad.astype(BF16)
    gsb[...] = signed.astype(BF16)
    gt[...] = jnp.transpose(grad).astype(BF16)
    gst[...] = jnp.transpose(signed).astype(BF16)

    def partials(first, stride, count):
        def one(i, carry):
            e = lax.rem(s + first + i * stride, NZ)
            t = columns(ta, e)
            gp[e, 0] = nn(gt[...], t).astype(BF16)
            gp[e, 1] = nn(gst[...], t * columns(sa, e)).astype(BF16)
            return carry

        lax.fori_loop(0, count, one, 0)

    def sum_out(way, left, m):
        e = lax.rem(s + (left if way == 0 else NZ - left), NZ)
        if left < 3 or (left == 3 and m == way):
            arrived(rr.at[way, left, m], rs_s.at[way, left, m], rs_r.at[way, left, m])
            gp[e, m] = (gp[e, m].astype(F32) + rr[way, left, m].astype(F32)).astype(BF16)
        start(
            gp.at[e, m], rr.at[way, left - 1, m], rs_s.at[way, left - 1, m], rs_r.at[way, left - 1, m],
            at_seq(1 if way == 0 else NZ - 1),
        )

    partials(4, 1, 1)
    sum_out(0, 4, 0)
    sum_out(1, 4, 1)
    partials(3, 2, 2)
    sum_out(0, 3, 1)
    sum_out(1, 3, 0)

    def back(e, carry):
        term = nt(gb[...], w_all[e, 0]) + columns(sa, e).astype(F32) * nt(gsb[...], w_all[e, 1])
        term = term.astype(BF16)
        row, first = lax.div(e, 2), 2 * lax.rem(e, 2)
        for j in range(4):
            bp[j % 2, row, first + j // 2] = term[:, j * DB : (j + 1) * DB]
        return carry

    for g in range(4):
        lax.fori_loop(2 * g, 2 * g + 2, back, 0)
        start(bp.at[oc, g], cr.at[g], bc_s.at[g], bc_r.at[g], partner)

    sum_out(0, 3, 0)
    sum_out(1, 3, 1)
    partials(NZ - 2, 1, 5)

    for g in range(4):
        arrived(cr.at[g], bc_s.at[g], bc_r.at[g])

    def join(i, carry):
        a, b = lax.div(i, 4), lax.rem(i, 4)
        bp[c, a, b] = (bp[c, a, b].astype(F32) + cr[a, b].astype(F32)).astype(BF16)
        return carry

    lax.fori_loop(0, 16, join, 0)
    top, low = pl.ds(0, HALF), pl.ds(HALF, HALF)
    for k in (1, 2, 3):
        start(bp.at[c, :, lax.rem(x + k, 4), top], xr.at[k - 1], bx_s.at[k - 1], bx_r.at[k - 1], at_x(k))
        start(bp.at[c, lax.rem(y + k, 4), :, low], yr.at[k - 1], by_s.at[k - 1], by_r.at[k - 1], at_y(k))

    sum_out(0, 2, 1)
    sum_out(1, 2, 0)
    sum_out(0, 2, 0)
    sum_out(1, 2, 1)

    for k in (1, 2, 3):
        arrived(xr.at[k - 1], bx_s.at[k - 1], bx_r.at[k - 1])
        arrived(yr.at[k - 1], by_s.at[k - 1], by_r.at[k - 1])
    for i in range(4):
        total = bp[c, i, x, top].astype(F32)
        other = bp[c, y, i, low].astype(F32)
        for k in range(3):
            total += xr[k, i].astype(F32)
            other += yr[k, i].astype(F32)
        xb[i] = total.astype(BF16)
        yb[i] = other.astype(BF16)
    for k in (1, 2, 3):
        start(xb.at[lax.rem(y + k, 4)], xr2.at[k - 1], by_s.at[2 + k], by_r.at[2 + k], at_y(k))
        start(yb.at[lax.rem(x + k, 4)], yr2.at[k - 1], bx_s.at[2 + k], bx_r.at[2 + k], at_x(k))

    sum_out(0, 1, 1)
    sum_out(1, 1, 0)

    for k in (1, 2, 3):
        arrived(xr2.at[k - 1], by_s.at[2 + k], by_r.at[2 + k])
        arrived(yr2.at[k - 1], bx_s.at[2 + k], bx_r.at[2 + k])
    total = xb[y].astype(F32)
    other = yb[x].astype(F32)
    for k in range(3):
        total += xr2[k].astype(F32)
        other += yr2[k].astype(F32)
    dtok_out[top, :] = total.astype(BF16)
    dtok_out[low, :] = other.astype(BF16)

    sum_out(0, 1, 0)
    sum_out(1, 1, 1)
    for m, out in ((1, gs_out), (0, gm_out)):
        for way in (0, 1):
            arrived(rr.at[way, 0, m], rs_s.at[way, 0, m], rs_r.at[way, 0, m])
        total = gp[s, m].astype(F32) + rr[0, 0, m].astype(F32) + rr[1, 0, m].astype(F32)
        out[...] = jnp.transpose(total).astype(BF16)

    for one in pending:
        one.wait_send()
    for k in range(1, NZ):
        @pl.when(s + k < NZ)
        def _():
            copy(sts, str_.at[k - 1], st_s.at[k - 1], st_r.at[k - 1], at_seq(k)).wait_send()

        @pl.when(s >= k)
        def _():
            copy(sus, sur.at[k - 1], su_s.at[k - 1], su_r.at[k - 1], at_seq(NZ - k)).wait_send()


def local(tokens, in_mask, out_mask, w_mean, w_sigma, grad_out):
    sgn = (2 * out_mask - 1).astype(BF16).reshape(TB, C)
    vm = pltpu.VMEM
    dma = pltpu.SemaphoreType.DMA
    attended, d_tokens, g_mean, g_sigma = pl.pallas_call(
        kernel,
        out_shape=(
            jax.ShapeDtypeStruct((TB, E), BF16),
            jax.ShapeDtypeStruct((TB, DB), BF16),
            jax.ShapeDtypeStruct((KB, C), BF16),
            jax.ShapeDtypeStruct((KB, C), BF16),
        ),
        in_specs=[pl.BlockSpec(memory_space=vm)] * 6,
        out_specs=[pl.BlockSpec(memory_space=vm)] * 4,
        scratch_shapes=[
            vm((2, 4, 4, TB, DB), BF16),
            vm((2, 4, 4, TB, DB), BF16),
            vm((NZ, 2, KB, C), BF16),
            vm((TB, C), F32),
            vm((TB, C), F32),
            vm((E, E), BF16),
            vm((NZ - 1, E, E), BF16),
            vm((E, E), BF16),
            vm((NZ - 1, E, E), BF16),
            vm((E, E), F32),
            vm((E, E), F32),
            vm((TB, TB), BF16),
            vm((TB, TB), BF16),
            vm((TB, TB), BF16),
            vm((TB, TB), BF16),
            vm((TB, E), F32),
            vm((TB, E), F32),
            vm((TB, E), F32),
            vm((TB, C), BF16),
            vm((TB, C), BF16),
            vm((C, TB), BF16),
            vm((C, TB), BF16),
            vm((NZ, 2, C, KB), BF16),
            vm((2, 4, 2, C, KB), BF16),
            vm((2, 4, 4, TB, DB), BF16),
            vm((4, 4, TB, DB), BF16),
            vm((3, 4, HALF, DB), BF16),
            vm((3, 4, HALF, DB), BF16),
            vm((4, HALF, DB), BF16),
            vm((4, HALF, DB), BF16),
            vm((3, HALF, DB), BF16),
            vm((3, HALF, DB), BF16),
            dma((2, 4, 2)), dma((2, 4, 2)),
            dma((6,)), dma((6,)),
            dma((6,)), dma((6,)),
            dma((8,)), dma((8,)),
            dma((7,)), dma((7,)),
            dma((7,)), dma((7,)),
            dma((2, 4, 2)), dma((2, 4, 2)),
            dma((4,)), dma((4,)),
            dma((6,)), dma((6,)),
            dma((6,)), dma((6,)),
        ],
        compiler_params=pltpu.CompilerParams(
            collective_id=0, has_side_effects=True, vmem_limit_bytes=56 * 1024 * 1024
        ),
        name="flipout_layer",
    )(tokens, in_mask, sgn, w_mean.reshape(KB, C), w_sigma.reshape(KB, C), grad_out)
    return attended, d_tokens, g_mean.reshape(KB, 1, C), g_sigma.reshape(KB, 1, C)


def solution(mesh):
    placed = (
        P("seq", "fsdp"),
        P("seq", "fsdp"),
        P("seq", "fsdp", None),
        P("seq", "fsdp", None),
        P("seq", "fsdp", None),
        P("seq", "fsdp"),
    )
    return jax.shard_map(
        local,
        mesh=mesh,
        in_specs=placed,
        out_specs=(P("seq", "fsdp"), P("seq", "fsdp"), P("seq", "fsdp", None), P("seq", "fsdp", None)),
        check_vma=False,
    )
```

```python
import jax
import jax.numpy as jnp
from jax import lax
from jax.experimental import pallas as pl
from jax.experimental.pallas import tpu as pltpu
from jax.sharding import PartitionSpec as P

EPSILON = 1e-06
MESH = pl.DeviceIdType.MESH
F32 = jnp.float32
BF16 = jnp.bfloat16
TB = 512
DB = 128
KB = 512
E = 128
C = 3 * E
NZ = 8
HALF = TB // 2
Q = TB // 4


def nn(a, b):
    return lax.dot_general(a, b, (((1,), (0,)), ((), ())), preferred_element_type=F32)


def nt(a, b):
    return lax.dot_general(a, b, (((1,), (1,)), ((), ())), preferred_element_type=F32)


def kernel(
    tok, in_mask, out_mask, w_mean, w_sigma, gout,
    att_out, dtok_out, gm_out, gs_out,
    ta, sa, sgn, w_all, pm, ps, sts, str_, sus, sur, inc, suf, sc, sct, ds, dst, nu, dki, dvi,
    gb, gsb, tq, t2, s2, so_all, gt_all, gmt, gst, bp, cr, xr, yr, xb, yb, xr2, yr2,
    zs, zr, ts, tr, ss, sr, cs, crs, st_s, st_r, su_s, su_r, q_s, q_r, z2_s, z2_r, t3_s, t3_r, s3_s, s3_r, c3_s, c3_r, so_s, so_r, g_s, g_r, bc_s, bc_r, bx_s, bx_r, by_s, by_r,
):
    s = lax.axis_index("seq")
    f = lax.axis_index("fsdp")
    c = lax.rem(f, 2)
    x = lax.rem(lax.div(f, 2), 4)
    y = lax.div(f, 8)
    oc = 1 - c

    def at_seq(k):
        return (lax.rem(s + k, NZ), f)

    def at_x(k):
        return (s, (y * 4 + lax.rem(x + k, 4)) * 2 + c)

    def at_y(k):
        return (s, (lax.rem(y + k, 4) * 4 + x) * 2 + c)

    def quarter(row):
        return pl.ds(pl.multiple_of(row * Q, Q), Q)

    side = lax.rem(x, 2)
    odd = lax.div(x, 2)
    holder = odd == lax.rem(s, 2)
    partner = (s, (y * 4 + x) * 2 + oc)
    pending = []

    def copy(src, dst, send, recv, dev):
        return pltpu.make_async_remote_copy(
            src_ref=src, dst_ref=dst, send_sem=send, recv_sem=recv, device_id=dev, device_id_type=MESH
        )

    def start(src, dst, send, recv, dev):
        one = copy(src, dst, send, recv, dev)
        one.start()
        pending.append(one)

    def arrived(ref, send, recv):
        copy(ref, ref, send, recv, partner).wait_recv()

    barrier = pltpu.get_barrier_semaphore()
    peers = [at_seq(k) for k in range(1, NZ)] + [at_x(k) for k in (1, 2, 3)] + [at_y(k) for k in (1, 2, 3)] + [partner]
    for peer in peers:
        pl.semaphore_signal(barrier, inc=1, device_id=peer, device_id_type=MESH)

    ta[c, y, x] = tok[...]
    tq[y] = tok[quarter(y), :]
    sa[c, y, x] = (2 * in_mask[...] - 1).astype(F32).astype(BF16)
    w_all[s, 0] = w_mean[...]
    w_all[s, 1] = w_sigma[...]
    pl.semaphore_wait(barrier, len(peers))

    def ring_out(way, hop, m):
        owner = lax.rem(s + (NZ - hop if way == 0 else hop), NZ)
        ref = w_all.at[owner, m]
        start(ref, ref, zs.at[way, hop, m], zr.at[way, hop, m], at_seq(1 if way == 0 else NZ - 1))

    def ring_in(way, hop, m):
        owner = lax.rem(s + (NZ - 1 - hop if way == 0 else 1 + hop), NZ)
        arrived(w_all.at[owner, m], zs.at[way, hop, m], zr.at[way, hop, m])

    def ring_step(hop, part):
        for way in (0, 1):
            m = part if way == 0 else 1 - part
            ring_in(way, hop, m)
            if hop < 2 or (hop == 2 and part == 0):
                ring_out(way, hop + 1, m)

    for part in (0, 1):
        ring_out(0, 0, part)
        ring_out(1, 0, 1 - part)

    def ring(ref_all, send, recv):
        def part(owner, way, hop):
            return ref_all.at[owner] if hop < 3 else ref_all.at[owner, pl.ds(way * (C // 2), C // 2)]

        def out(hop):
            for way in (0, 1):
                ref = part(lax.rem(s + (NZ - hop if way == 0 else hop), NZ), way, hop)
                start(ref, ref, send.at[way, hop], recv.at[way, hop], at_seq(1 if way == 0 else NZ - 1))

        def step(hop):
            for way in (0, 1):
                owner = lax.rem(s + (NZ - 1 - hop if way == 0 else 1 + hop), NZ)
                arrived(part(owner, way, hop), send.at[way, hop], recv.at[way, hop])
            if hop < 3:
                out(hop + 1)

        return out, step

    so_out, so_step = ring(so_all, so_s, so_r)
    g_out, g_step = ring(gt_all, g_s, g_r)

    for k in (1, 2, 3):
        start(ta.at[c, y, x], ta.at[c, y, x], ts.at[k - 1], tr.at[k - 1], at_x(k))
        start(sa.at[c, y, x], sa.at[c, y, x], ss.at[k - 1], sr.at[k - 1], at_y(k))
        start(ta.at[c, y, x, quarter(lax.rem(y + k, 4))], tq.at[y], q_s.at[k - 1], q_r.at[k - 1], at_y(k))
    for k in (1, 2, 3):
        arrived(ta.at[c, y, lax.rem(x + 4 - k, 4)], ts.at[k - 1], tr.at[k - 1])
    for k in (1, 2, 3):
        start(ta.at[c, y], ta.at[c, y], ts.at[2 + k], tr.at[2 + k], at_y(k))
    for k in (1, 2, 3):
        arrived(sa.at[c, lax.rem(y + 4 - k, 4), x], ss.at[k - 1], sr.at[k - 1])
    for k in (1, 2, 3):
        start(sa.at[c, :, x], sa.at[c, :, x], ss.at[2 + k], sr.at[2 + k], at_x(k))
    start(ta.at[c, y], ta.at[c, y], cs.at[0], crs.at[0], partner)
    start(sa.at[c, :, x], sa.at[c, :, x], cs.at[4], crs.at[4], partner)

    for k in (1, 2, 3):
        arrived(tq.at[lax.rem(y + 4 - k, 4)], q_s.at[k - 1], q_r.at[k - 1])

    def to_planes(act):
        for row in range(4):
            plane = 2 * row + odd

            @pl.when(plane != s)
            def _():
                act(copy(tq.at[row], t2.at[c, y, side, s], z2_s.at[0, row], z2_r.at[0, s], (plane, f)))
                act(copy(sa.at[c, row, x, quarter(y)], s2.at[c, y, side, s], z2_s.at[1, row], z2_r.at[1, s], (plane, f)))

    to_planes(lambda one: one.start())

    @pl.when(holder)
    def _():
        t2[c, y, side, s] = tq[lax.div(s, 2)]
        s2[c, y, side, s] = sa[c, lax.div(s, 2), x, quarter(y), :]

    def spread_first(act):
        for k in (1, 2, 3):
            act(copy(t2.at[c, y, side], t2.at[c, y, side], t3_s.at[k - 1], t3_r.at[side], at_x(k)))
            act(copy(s2.at[c, y, side], s2.at[c, y, side], s3_s.at[k - 1], s3_r.at[k - 1], at_y(k)))

    def spread_signs(act):
        for k in (1, 2, 3):
            act(copy(s2.at[c, :, side], s2.at[c, :, side], s3_s.at[2 + k], s3_r.at[3 + side], at_x(k)))

    def from_holders(ref_of, send, recv):
        for b in (0, 1):
            @pl.when(2 * lax.rem(s, 2) + b != x)
            def _():
                arrived(ref_of(b), send, recv(b))

    sgn[...] = (2 * out_mask[:, 0, :] - 1).astype(F32)
    so_all[s] = jnp.transpose(sgn[...]).astype(BF16)
    ring_step(0, 0)
    ring_step(0, 1)
    ring_step(1, 0)
    for k in (1, 2, 3):
        yk = lax.rem(y + 4 - k, 4)
        arrived(ta.at[c, yk], ts.at[2 + k], tr.at[2 + k])
        start(ta.at[c, yk], ta.at[c, yk], cs.at[k], crs.at[k], partner)
        xk = lax.rem(x + 4 - k, 4)
        arrived(sa.at[c, :, xk], ss.at[2 + k], sr.at[2 + k])
        start(sa.at[c, :, xk], sa.at[c, :, xk], cs.at[4 + k], crs.at[4 + k], partner)
    @pl.when(holder)
    def _():
        for k in range(1, NZ):
            source = lax.rem(s + k, NZ)
            arrived(t2.at[c, y, side, source], z2_s.at[0, 0], z2_r.at[0, source])
            arrived(s2.at[c, y, side, source], z2_s.at[1, 0], z2_r.at[1, source])
        spread_first(lambda one: one.start())

    ring_step(1, 1)
    for k in range(4):
        arrived(ta.at[oc, lax.rem(y + 4 - k, 4)], cs.at[k], crs.at[k])
        arrived(sa.at[oc, :, lax.rem(x + 4 - k, 4)], cs.at[4 + k], crs.at[4 + k])

    def columns(ref, e):
        row, first = lax.div(e, 2), 2 * lax.rem(e, 2)
        return jnp.concatenate([ref[j % 2, row, first + j // 2] for j in range(4)], axis=1)

    pm[...] = jnp.zeros_like(pm)
    ps[...] = jnp.zeros_like(ps)

    def project(first, stride, count):
        def one(i, carry):
            owner = lax.rem(s + first + i * stride, NZ)
            t = columns(ta, owner)
            pm[...] += nn(t, w_all[owner, 0])
            ps[...] += nn(t * columns(sa, owner), w_all[owner, 1])
            return carry

        lax.fori_loop(0, count, one, 0)

    project(NZ - 2, 1, 5)
    ring_step(2, 0)
    from_holders(lambda b: t2.at[c, y, b], t3_s.at[0], lambda b: t3_r.at[b])
    for k in (1, 2, 3):
        start(t2.at[c, y], t2.at[c, y], t3_s.at[2 + k], t3_r.at[1 + k], at_y(k))

    @pl.when(holder)
    def _():
        for k in (1, 2, 3):
            arrived(s2.at[c, lax.rem(y + 4 - k, 4), side], s3_s.at[k - 1], s3_r.at[k - 1])
        spread_signs(lambda one: one.start())

    ring_step(2, 1)
    project(NZ - 3, 6, 2)
    ring_in(0, 3, 0)
    ring_in(1, 3, 1)
    so_out(0)
    project(4, 1, 1)

    so = sgn[...]
    pre = pm[...] + ps[...] * so
    uq, uk, v = pre[:, :E], pre[:, E : 2 * E], pre[:, 2 * E :]
    exp_q, exp_k = jnp.exp(jnp.minimum(uq, 0.0)), jnp.exp(jnp.minimum(uk, 0.0))
    q = jnp.where(uq > 0, uq + 1.0, exp_q)
    kf = jnp.where(uk > 0, uk + 1.0, exp_k)
    slope_q = jnp.where(uq > 0, 1.0, exp_q)
    slope_k = jnp.where(uk > 0, 1.0, exp_k)
    qb, kb, vb = q.astype(BF16), kf.astype(BF16), v.astype(BF16)

    sts[...] = nn(jnp.transpose(kf).astype(BF16), vb).astype(BF16)
    for k in range(1, NZ):
        @pl.when(s + k < NZ)
        def _():
            copy(sts, str_.at[k - 1], st_s.at[k - 1], st_r.at[k - 1], at_seq(k)).start()

    rows = lax.broadcasted_iota(jnp.int32, (TB, TB), 0)
    cols = lax.broadcasted_iota(jnp.int32, (TB, TB), 1)
    sc[...] = jnp.where(rows >= cols, nt(qb, kb), 0.0).astype(BF16)
    sct[...] = jnp.where(rows <= cols, nt(kb, qb), 0.0).astype(BF16)
    nu[...] = nn(sc[...], vb)
    inc[...] = jnp.zeros_like(inc)
    for k in (1, 2, 3):
        arrived(t2.at[c, lax.rem(y + 4 - k, 4)], t3_s.at[2 + k], t3_r.at[1 + k])
    from_holders(lambda b: s2.at[c, :, b], s3_s.at[3], lambda b: s3_r.at[3 + b])
    for k in range(4):
        start(t2.at[c, k], t2.at[c, k], c3_s.at[k], c3_r.at[k], partner)
    for b in range(2):
        start(s2.at[c, :, b], s2.at[c, :, b], c3_s.at[4 + b], c3_r.at[4 + b], partner)
    for k in range(1, NZ):
        @pl.when(s >= k)
        def _():
            arrived(str_.at[k - 1], st_s.at[k - 1], st_r.at[k - 1])
            inc[...] += str_[k - 1].astype(F32)

    inb = inc[...].astype(BF16)
    num = nu[...] + nn(qb, inb)
    inv = lax.rsqrt(jnp.mean(num * num, axis=-1, keepdims=True) + EPSILON)
    normed = num * inv
    att_out[...] = normed.astype(BF16)
    up = gout[...].astype(F32)
    dn = inv * (up - normed * jnp.mean(up * normed, axis=-1, keepdims=True))
    dnb = dn.astype(BF16)
    sus[...] = nn(jnp.transpose(q).astype(BF16), dnb).astype(BF16)
    for k in range(1, NZ):
        @pl.when(s >= k)
        def _():
            copy(sus, sur.at[k - 1], su_s.at[k - 1], su_r.at[k - 1], at_seq(NZ - k)).start()

    ds[...] = jnp.where(rows >= cols, nt(dnb, vb), 0.0).astype(BF16)
    dst[...] = jnp.where(rows <= cols, nt(vb, dnb), 0.0).astype(BF16)
    dq = (nn(ds[...], kb) + nt(dnb, inb)) * slope_q
    dki[...] = nn(dst[...], qb)
    dvi[...] = nn(sct[...], dnb)
    suf[...] = jnp.zeros_like(suf)
    so_step(0)
    for k in range(1, NZ):
        @pl.when(s + k < NZ)
        def _():
            arrived(sur.at[k - 1], su_s.at[k - 1], su_r.at[k - 1])
            suf[...] += sur[k - 1].astype(F32)

    sfb = suf[...].astype(BF16)
    dk = (dki[...] + nt(vb, sfb)) * slope_k
    dv = dvi[...] + nn(kb, sfb)
    grad = jnp.concatenate([dq, dk, dv], axis=1)
    signed = grad * so
    gt_all[s] = jnp.transpose(grad).astype(BF16)
    g_out(0)
    gb[...] = grad.astype(BF16)
    gsb[...] = signed.astype(BF16)
    so_step(1)

    gmt[...] = jnp.zeros_like(gmt)
    gst[...] = jnp.zeros_like(gst)

    def block(ref, owner):
        return jnp.concatenate([ref[j % 2, :, j // 2, owner].reshape(TB, DB) for j in range(4)], axis=1)

    def gather_grads(first, stride, count):
        def one(i, carry):
            owner = lax.rem(s + first + i * stride, NZ)
            t, g = block(t2, owner), gt_all[owner]
            gmt[...] += nn(g, t)
            gst[...] += nn(g * so_all[owner], t * block(s2, owner))
            return carry

        lax.fori_loop(0, count, one, 0)

    def back(e, carry):
        term = nt(gb[...], w_all[e, 0]) + columns(sa, e).astype(F32) * nt(gsb[...], w_all[e, 1])
        term = term.astype(BF16)
        row, first = lax.div(e, 2), 2 * lax.rem(e, 2)
        for j in range(4):
            bp[j % 2, row, first + j // 2] = term[:, j * DB : (j + 1) * DB]
        return carry

    for g in range(4):
        lax.fori_loop(2 * g, 2 * g + 2, back, 0)
        start(bp.at[oc, g], cr.at[g], bc_s.at[g], bc_r.at[g], partner)

    for k in range(4):
        arrived(t2.at[oc, k], c3_s.at[k], c3_r.at[k])
    for b in range(2):
        arrived(s2.at[oc, :, b], c3_s.at[4 + b], c3_r.at[4 + b])
    gather_grads(0, 1, 1)
    g_step(0)
    so_step(2)

    for g in range(4):
        arrived(cr.at[g], bc_s.at[g], bc_r.at[g])

    def join(i, carry):
        a, b = lax.div(i, 4), lax.rem(i, 4)
        bp[c, a, b] = (bp[c, a, b].astype(F32) + cr[a, b].astype(F32)).astype(BF16)
        return carry

    lax.fori_loop(0, 16, join, 0)
    top, low = pl.ds(0, HALF), pl.ds(HALF, HALF)
    for k in (1, 2, 3):
        start(bp.at[c, :, lax.rem(x + k, 4), top], xr.at[k - 1], bx_s.at[k - 1], bx_r.at[k - 1], at_x(k))
        start(bp.at[c, lax.rem(y + k, 4), :, low], yr.at[k - 1], by_s.at[k - 1], by_r.at[k - 1], at_y(k))

    gather_grads(1, 6, 2)
    g_step(1)

    for k in (1, 2, 3):
        arrived(xr.at[k - 1], bx_s.at[k - 1], bx_r.at[k - 1])
        arrived(yr.at[k - 1], by_s.at[k - 1], by_r.at[k - 1])
    for i in range(4):
        total = bp[c, i, x, top].astype(F32)
        other = bp[c, y, i, low].astype(F32)
        for k in range(3):
            total += xr[k, i].astype(F32)
            other += yr[k, i].astype(F32)
        xb[i] = total.astype(BF16)
        yb[i] = other.astype(BF16)
    for k in (1, 2, 3):
        start(xb.at[lax.rem(y + k, 4)], xr2.at[k - 1], by_s.at[2 + k], by_r.at[2 + k], at_y(k))
        start(yb.at[lax.rem(x + k, 4)], yr2.at[k - 1], bx_s.at[2 + k], bx_r.at[2 + k], at_x(k))

    gather_grads(2, 4, 2)
    g_step(2)
    so_step(3)

    for k in (1, 2, 3):
        arrived(xr2.at[k - 1], by_s.at[2 + k], by_r.at[2 + k])
        arrived(yr2.at[k - 1], bx_s.at[2 + k], bx_r.at[2 + k])
    total = xb[y].astype(F32)
    other = yb[x].astype(F32)
    for k in range(3):
        total += xr2[k].astype(F32)
        other += yr2[k].astype(F32)
    dtok_out[top, :] = total.astype(BF16)
    dtok_out[low, :] = other.astype(BF16)

    gather_grads(3, 2, 2)
    g_step(3)
    gather_grads(4, 1, 1)
    gm_out[...] = jnp.transpose(gmt[...]).astype(BF16)
    gs_out[...] = jnp.transpose(gst[...]).astype(BF16)

    to_planes(lambda one: one.wait_send())

    @pl.when(holder)
    def _():
        spread_first(lambda one: one.wait_send())
        spread_signs(lambda one: one.wait_send())

    for one in pending:
        one.wait_send()
    for k in range(1, NZ):
        @pl.when(s + k < NZ)
        def _():
            copy(sts, str_.at[k - 1], st_s.at[k - 1], st_r.at[k - 1], at_seq(k)).wait_send()

        @pl.when(s >= k)
        def _():
            copy(sus, sur.at[k - 1], su_s.at[k - 1], su_r.at[k - 1], at_seq(NZ - k)).wait_send()


def hand_over(*refs):
    n = len(refs) // 2
    copies = [pltpu.make_async_copy(refs[i], refs[n + i], refs[2 * n].at[i]) for i in range(n)]
    for one in copies:
        one.start()
    for one in copies:
        one.wait()


def local(tokens, in_mask, out_mask, w_mean, w_sigma, grad_out):
    vm = pltpu.VMEM
    dma = pltpu.SemaphoreType.DMA
    results = pl.pallas_call(
        kernel,
        out_shape=(
            jax.ShapeDtypeStruct((TB, E), BF16),
            jax.ShapeDtypeStruct((TB, DB), BF16),
            jax.ShapeDtypeStruct((KB, C), BF16),
            jax.ShapeDtypeStruct((KB, C), BF16),
        ),
        in_specs=[pl.BlockSpec(memory_space=vm)] * 6,
        out_specs=[pl.BlockSpec(memory_space=vm)] * 4,
        scratch_shapes=[
            vm((2, 4, 4, TB, DB), BF16),
            vm((2, 4, 4, TB, DB), BF16),
            vm((TB, C), F32),
            vm((NZ, 2, KB, C), BF16),
            vm((TB, C), F32),
            vm((TB, C), F32),
            vm((E, E), BF16),
            vm((NZ - 1, E, E), BF16),
            vm((E, E), BF16),
            vm((NZ - 1, E, E), BF16),
            vm((E, E), F32),
            vm((E, E), F32),
            vm((TB, TB), BF16),
            vm((TB, TB), BF16),
            vm((TB, TB), BF16),
            vm((TB, TB), BF16),
            vm((TB, E), F32),
            vm((TB, E), F32),
            vm((TB, E), F32),
            vm((TB, C), BF16),
            vm((TB, C), BF16),
            vm((4, Q, DB), BF16),
            vm((2, 4, 2, NZ, Q, DB), BF16),
            vm((2, 4, 2, NZ, Q, DB), BF16),
            vm((NZ, C, TB), BF16),
            vm((NZ, C, TB), BF16),
            vm((C, KB), F32),
            vm((C, KB), F32),
            vm((2, 4, 4, TB, DB), BF16),
            vm((4, 4, TB, DB), BF16),
            vm((3, 4, HALF, DB), BF16),
            vm((3, 4, HALF, DB), BF16),
            vm((4, HALF, DB), BF16),
            vm((4, HALF, DB), BF16),
            vm((3, HALF, DB), BF16),
            vm((3, HALF, DB), BF16),
            dma((2, 4, 2)), dma((2, 4, 2)),
            dma((6,)), dma((6,)),
            dma((6,)), dma((6,)),
            dma((8,)), dma((8,)),
            dma((7,)), dma((7,)),
            dma((7,)), dma((7,)),
            dma((3,)), dma((3,)),
            dma((2, 4)), dma((2, NZ)),
            dma((6,)), dma((5,)),
            dma((6,)), dma((5,)),
            dma((6,)), dma((6,)),
            dma((2, 4)), dma((2, 4)),
            dma((2, 4)), dma((2, 4)),
            dma((4,)), dma((4,)),
            dma((6,)), dma((6,)),
            dma((6,)), dma((6,)),
        ],
        compiler_params=pltpu.CompilerParams(
            collective_id=0, has_side_effects=True, vmem_limit_bytes=56 * 1024 * 1024
        ),
        name="flipout_layer",
    )(tokens, in_mask, out_mask, w_mean.reshape(KB, C), w_sigma.reshape(KB, C), grad_out)
    attended, d_tokens, g_mean, g_sigma = pl.pallas_call(
        hand_over,
        out_shape=[jax.ShapeDtypeStruct(r.shape, r.dtype) for r in results],
        in_specs=[pl.BlockSpec(memory_space=pl.ANY)] * 4,
        out_specs=[pl.BlockSpec(memory_space=vm)] * 4,
        scratch_shapes=[dma((4,))],
        name="hand_over",
    )(*results)
    return attended, d_tokens, g_mean.reshape(KB, 1, C), g_sigma.reshape(KB, 1, C)


def solution(mesh):
    placed = (
        P("seq", "fsdp"),
        P("seq", "fsdp"),
        P("seq", "fsdp", None),
        P("seq", "fsdp", None),
        P("seq", "fsdp", None),
        P("seq", "fsdp"),
    )
    return jax.shard_map(
        local,
        mesh=mesh,
        in_specs=placed,
        out_specs=(P("seq", "fsdp"), P("seq", "fsdp"), P("seq", "fsdp", None), P("seq", "fsdp", None)),
        check_vma=False,
    )
```

```python
import jax
import jax.numpy as jnp
from jax import lax
from jax.experimental import pallas as pl
from jax.experimental.pallas import tpu as pltpu
from jax.sharding import PartitionSpec as P

EPSILON = 1e-06
MESH = pl.DeviceIdType.MESH
F32 = jnp.float32
BF16 = jnp.bfloat16
TB = 512
DB = 128
KB = 512
E = 128
C = 3 * E
NZ = 8
HALF = TB // 2


def nn(a, b):
    return lax.dot_general(a, b, (((1,), (0,)), ((), ())), preferred_element_type=F32)


def nt(a, b):
    return lax.dot_general(a, b, (((1,), (1,)), ((), ())), preferred_element_type=F32)


def kernel(
    tok, in_mask, out_mask, w_mean, w_sigma, gout,
    att_out, dtok_out, gm_out, gs_out,
    ta, sa, sgn, w_all, pm, ps, sts, str_, sus, sur, inc, suf, sc, sct, ds, dst, nu, dki, dvi,
    gb, gsb, gt, gst, gp, rr, bp, cr, xr, yr, xb, yb, xr2, yr2,
    zs, zr, ts, tr, ss, sr, cs, crs, st_s, st_r, su_s, su_r, rs_s, rs_r, bc_s, bc_r, bx_s, bx_r, by_s, by_r,
):
    s = lax.axis_index("seq")
    f = lax.axis_index("fsdp")
    c = lax.rem(f, 2)
    x = lax.rem(lax.div(f, 2), 4)
    y = lax.div(f, 8)
    oc = 1 - c

    def at_seq(k):
        return (lax.rem(s + k, NZ), f)

    def at_x(k):
        return (s, (y * 4 + lax.rem(x + k, 4)) * 2 + c)

    def at_y(k):
        return (s, (lax.rem(y + k, 4) * 4 + x) * 2 + c)

    partner = (s, (y * 4 + x) * 2 + oc)
    pending = []

    def copy(src, dst, send, recv, dev):
        return pltpu.make_async_remote_copy(
            src_ref=src, dst_ref=dst, send_sem=send, recv_sem=recv, device_id=dev, device_id_type=MESH
        )

    def start(src, dst, send, recv, dev):
        one = copy(src, dst, send, recv, dev)
        one.start()
        pending.append(one)

    def arrived(ref, send, recv):
        copy(ref, ref, send, recv, partner).wait_recv()

    barrier = pltpu.get_barrier_semaphore()
    peers = [at_seq(k) for k in range(1, NZ)] + [at_x(k) for k in (1, 2, 3)] + [at_y(k) for k in (1, 2, 3)] + [partner]
    for peer in peers:
        pl.semaphore_signal(barrier, inc=1, device_id=peer, device_id_type=MESH)

    ta[c, y, x] = tok[...]
    sa[c, y, x] = (2 * in_mask[...] - 1).astype(F32).astype(BF16)
    w_all[s, 0] = w_mean[...]
    w_all[s, 1] = w_sigma[...]
    pl.semaphore_wait(barrier, len(peers))

    def ring_out(way, hop, m):
        owner = lax.rem(s + (NZ - hop if way == 0 else hop), NZ)
        ref = w_all.at[owner, m]
        start(ref, ref, zs.at[way, hop, m], zr.at[way, hop, m], at_seq(1 if way == 0 else NZ - 1))

    def ring_in(way, hop, m):
        owner = lax.rem(s + (NZ - 1 - hop if way == 0 else 1 + hop), NZ)
        arrived(w_all.at[owner, m], zs.at[way, hop, m], zr.at[way, hop, m])

    def ring_step(hop, part):
        for way in (0, 1):
            m = part if way == 0 else 1 - part
            ring_in(way, hop, m)
            if hop < 2 or (hop == 2 and part == 0):
                ring_out(way, hop + 1, m)

    for part in (0, 1):
        ring_out(0, 0, part)
        ring_out(1, 0, 1 - part)

    for k in (1, 2, 3):
        start(ta.at[c, y, x], ta.at[c, y, x], ts.at[k - 1], tr.at[k - 1], at_x(k))
        start(sa.at[c, y, x], sa.at[c, y, x], ss.at[k - 1], sr.at[k - 1], at_y(k))
    for k in (1, 2, 3):
        arrived(ta.at[c, y, lax.rem(x + 4 - k, 4)], ts.at[k - 1], tr.at[k - 1])
    for k in (1, 2, 3):
        start(ta.at[c, y], ta.at[c, y], ts.at[2 + k], tr.at[2 + k], at_y(k))
    for k in (1, 2, 3):
        arrived(sa.at[c, lax.rem(y + 4 - k, 4), x], ss.at[k - 1], sr.at[k - 1])
    for k in (1, 2, 3):
        start(sa.at[c, :, x], sa.at[c, :, x], ss.at[2 + k], sr.at[2 + k], at_x(k))
    start(ta.at[c, y], ta.at[c, y], cs.at[0], crs.at[0], partner)
    start(sa.at[c, :, x], sa.at[c, :, x], cs.at[4], crs.at[4], partner)

    sgn[...] = (2 * out_mask[:, 0, :] - 1).astype(F32)
    ring_step(0, 0)
    ring_step(0, 1)
    ring_step(1, 0)
    for k in (1, 2, 3):
        yk = lax.rem(y + 4 - k, 4)
        arrived(ta.at[c, yk], ts.at[2 + k], tr.at[2 + k])
        start(ta.at[c, yk], ta.at[c, yk], cs.at[k], crs.at[k], partner)
        xk = lax.rem(x + 4 - k, 4)
        arrived(sa.at[c, :, xk], ss.at[2 + k], sr.at[2 + k])
        start(sa.at[c, :, xk], sa.at[c, :, xk], cs.at[4 + k], crs.at[4 + k], partner)
    ring_step(1, 1)
    for k in range(4):
        arrived(ta.at[oc, lax.rem(y + 4 - k, 4)], cs.at[k], crs.at[k])
        arrived(sa.at[oc, :, lax.rem(x + 4 - k, 4)], cs.at[4 + k], crs.at[4 + k])

    def columns(ref, e):
        row, first = lax.div(e, 2), 2 * lax.rem(e, 2)
        return jnp.concatenate([ref[j % 2, row, first + j // 2] for j in range(4)], axis=1)

    pm[...] = jnp.zeros_like(pm)
    ps[...] = jnp.zeros_like(ps)

    def project(first, stride, count):
        def one(i, carry):
            owner = lax.rem(s + first + i * stride, NZ)
            t = columns(ta, owner)
            pm[...] += nn(t, w_all[owner, 0])
            ps[...] += nn(t * columns(sa, owner), w_all[owner, 1])
            return carry

        lax.fori_loop(0, count, one, 0)

    project(NZ - 2, 1, 5)
    ring_step(2, 0)
    ring_step(2, 1)
    project(NZ - 3, 6, 2)
    ring_in(0, 3, 0)
    ring_in(1, 3, 1)
    project(4, 1, 1)

    so = sgn[...]
    pre = pm[...] + ps[...] * so
    uq, uk, v = pre[:, :E], pre[:, E : 2 * E], pre[:, 2 * E :]
    exp_q, exp_k = jnp.exp(jnp.minimum(uq, 0.0)), jnp.exp(jnp.minimum(uk, 0.0))
    q = jnp.where(uq > 0, uq + 1.0, exp_q)
    kf = jnp.where(uk > 0, uk + 1.0, exp_k)
    slope_q = jnp.where(uq > 0, 1.0, exp_q)
    slope_k = jnp.where(uk > 0, 1.0, exp_k)
    qb, kb, vb = q.astype(BF16), kf.astype(BF16), v.astype(BF16)

    sts[...] = nn(jnp.transpose(kf).astype(BF16), vb).astype(BF16)
    for k in range(1, NZ):
        @pl.when(s + k < NZ)
        def _():
            copy(sts, str_.at[k - 1], st_s.at[k - 1], st_r.at[k - 1], at_seq(k)).start()

    rows = lax.broadcasted_iota(jnp.int32, (TB, TB), 0)
    cols = lax.broadcasted_iota(jnp.int32, (TB, TB), 1)
    sc[...] = jnp.where(rows >= cols, nt(qb, kb), 0.0).astype(BF16)
    sct[...] = jnp.where(rows <= cols, nt(kb, qb), 0.0).astype(BF16)
    nu[...] = nn(sc[...], vb)
    inc[...] = jnp.zeros_like(inc)
    for k in range(1, NZ):
        @pl.when(s >= k)
        def _():
            arrived(str_.at[k - 1], st_s.at[k - 1], st_r.at[k - 1])
            inc[...] += str_[k - 1].astype(F32)

    inb = inc[...].astype(BF16)
    num = nu[...] + nn(qb, inb)
    inv = lax.rsqrt(jnp.mean(num * num, axis=-1, keepdims=True) + EPSILON)
    normed = num * inv
    att_out[...] = normed.astype(BF16)
    up = gout[...].astype(F32)
    dn = inv * (up - normed * jnp.mean(up * normed, axis=-1, keepdims=True))
    dnb = dn.astype(BF16)
    sus[...] = nn(jnp.transpose(q).astype(BF16), dnb).astype(BF16)
    for k in range(1, NZ):
        @pl.when(s >= k)
        def _():
            copy(sus, sur.at[k - 1], su_s.at[k - 1], su_r.at[k - 1], at_seq(NZ - k)).start()

    ds[...] = jnp.where(rows >= cols, nt(dnb, vb), 0.0).astype(BF16)
    dst[...] = jnp.where(rows <= cols, nt(vb, dnb), 0.0).astype(BF16)
    dq = (nn(ds[...], kb) + nt(dnb, inb)) * slope_q
    dki[...] = nn(dst[...], qb)
    dvi[...] = nn(sct[...], dnb)
    suf[...] = jnp.zeros_like(suf)
    for k in range(1, NZ):
        @pl.when(s + k < NZ)
        def _():
            arrived(sur.at[k - 1], su_s.at[k - 1], su_r.at[k - 1])
            suf[...] += sur[k - 1].astype(F32)

    sfb = suf[...].astype(BF16)
    dk = (dki[...] + nt(vb, sfb)) * slope_k
    dv = dvi[...] + nn(kb, sfb)
    grad = jnp.concatenate([dq, dk, dv], axis=1)
    signed = grad * so
    gb[...] = grad.astype(BF16)
    gsb[...] = signed.astype(BF16)
    gt[...] = jnp.transpose(grad).astype(BF16)
    gst[...] = jnp.transpose(signed).astype(BF16)

    def partials(first, stride, count):
        def one(i, carry):
            e = lax.rem(s + first + i * stride, NZ)
            t = columns(ta, e)
            gp[e, 0] = nn(gt[...], t).astype(BF16)
            gp[e, 1] = nn(gst[...], t * columns(sa, e)).astype(BF16)
            return carry

        lax.fori_loop(0, count, one, 0)

    def sum_out(way, left, m):
        e = lax.rem(s + (left if way == 0 else NZ - left), NZ)
        if left < 3 or (left == 3 and m == way):
            arrived(rr.at[way, left, m], rs_s.at[way, left, m], rs_r.at[way, left, m])
            gp[e, m] = (gp[e, m].astype(F32) + rr[way, left, m].astype(F32)).astype(BF16)
        start(
            gp.at[e, m], rr.at[way, left - 1, m], rs_s.at[way, left - 1, m], rs_r.at[way, left - 1, m],
            at_seq(1 if way == 0 else NZ - 1),
        )

    partials(4, 1, 1)
    sum_out(0, 4, 0)
    sum_out(1, 4, 1)
    partials(3, 2, 2)
    sum_out(0, 3, 1)
    sum_out(1, 3, 0)

    def back(e, carry):
        term = nt(gb[...], w_all[e, 0]) + columns(sa, e).astype(F32) * nt(gsb[...], w_all[e, 1])
        term = term.astype(BF16)
        row, first = lax.div(e, 2), 2 * lax.rem(e, 2)
        for j in range(4):
            bp[j % 2, row, first + j // 2] = term[:, j * DB : (j + 1) * DB]
        return carry

    for g in range(4):
        lax.fori_loop(2 * g, 2 * g + 2, back, 0)
        start(bp.at[oc, g], cr.at[g], bc_s.at[g], bc_r.at[g], partner)

    sum_out(0, 3, 0)
    sum_out(1, 3, 1)
    partials(NZ - 2, 1, 5)

    for g in range(4):
        arrived(cr.at[g], bc_s.at[g], bc_r.at[g])

    def join(i, carry):
        a, b = lax.div(i, 4), lax.rem(i, 4)
        bp[c, a, b] = (bp[c, a, b].astype(F32) + cr[a, b].astype(F32)).astype(BF16)
        return carry

    lax.fori_loop(0, 16, join, 0)
    top, low = pl.ds(0, HALF), pl.ds(HALF, HALF)
    for k in (1, 2, 3):
        start(bp.at[c, :, lax.rem(x + k, 4), top], xr.at[k - 1], bx_s.at[k - 1], bx_r.at[k - 1], at_x(k))
        start(bp.at[c, lax.rem(y + k, 4), :, low], yr.at[k - 1], by_s.at[k - 1], by_r.at[k - 1], at_y(k))

    sum_out(0, 2, 1)
    sum_out(1, 2, 0)
    sum_out(0, 2, 0)
    sum_out(1, 2, 1)

    for k in (1, 2, 3):
        arrived(xr.at[k - 1], bx_s.at[k - 1], bx_r.at[k - 1])
        arrived(yr.at[k - 1], by_s.at[k - 1], by_r.at[k - 1])
    for i in range(4):
        total = bp[c, i, x, top].astype(F32)
        other = bp[c, y, i, low].astype(F32)
        for k in range(3):
            total += xr[k, i].astype(F32)
            other += yr[k, i].astype(F32)
        xb[i] = total.astype(BF16)
        yb[i] = other.astype(BF16)
    for k in (1, 2, 3):
        start(xb.at[lax.rem(y + k, 4)], xr2.at[k - 1], by_s.at[2 + k], by_r.at[2 + k], at_y(k))
        start(yb.at[lax.rem(x + k, 4)], yr2.at[k - 1], bx_s.at[2 + k], bx_r.at[2 + k], at_x(k))

    sum_out(0, 1, 1)
    sum_out(1, 1, 0)

    for k in (1, 2, 3):
        arrived(xr2.at[k - 1], by_s.at[2 + k], by_r.at[2 + k])
        arrived(yr2.at[k - 1], bx_s.at[2 + k], bx_r.at[2 + k])
    total = xb[y].astype(F32)
    other = yb[x].astype(F32)
    for k in range(3):
        total += xr2[k].astype(F32)
        other += yr2[k].astype(F32)
    dtok_out[top, :] = total.astype(BF16)
    dtok_out[low, :] = other.astype(BF16)

    sum_out(0, 1, 0)
    sum_out(1, 1, 1)
    for m, out in ((1, gs_out), (0, gm_out)):
        for way in (0, 1):
            arrived(rr.at[way, 0, m], rs_s.at[way, 0, m], rs_r.at[way, 0, m])
        total = gp[s, m].astype(F32) + rr[0, 0, m].astype(F32) + rr[1, 0, m].astype(F32)
        out[...] = jnp.transpose(total).astype(BF16)

    for one in pending:
        one.wait_send()
    for k in range(1, NZ):
        @pl.when(s + k < NZ)
        def _():
            copy(sts, str_.at[k - 1], st_s.at[k - 1], st_r.at[k - 1], at_seq(k)).wait_send()

        @pl.when(s >= k)
        def _():
            copy(sus, sur.at[k - 1], su_s.at[k - 1], su_r.at[k - 1], at_seq(NZ - k)).wait_send()


def hand_over(*refs):
    n = len(refs) // 2
    copies = [pltpu.make_async_copy(refs[i], refs[n + i], refs[2 * n].at[i]) for i in range(n)]
    for one in copies:
        one.start()
    for one in copies:
        one.wait()


def local(tokens, in_mask, out_mask, w_mean, w_sigma, grad_out):
    vm = pltpu.VMEM
    dma = pltpu.SemaphoreType.DMA
    results = pl.pallas_call(
        kernel,
        out_shape=(
            jax.ShapeDtypeStruct((TB, E), BF16),
            jax.ShapeDtypeStruct((TB, DB), BF16),
            jax.ShapeDtypeStruct((KB, C), BF16),
            jax.ShapeDtypeStruct((KB, C), BF16),
        ),
        in_specs=[pl.BlockSpec(memory_space=vm)] * 6,
        out_specs=[pl.BlockSpec(memory_space=vm)] * 4,
        scratch_shapes=[
            vm((2, 4, 4, TB, DB), BF16),
            vm((2, 4, 4, TB, DB), BF16),
            vm((TB, C), F32),
            vm((NZ, 2, KB, C), BF16),
            vm((TB, C), F32),
            vm((TB, C), F32),
            vm((E, E), BF16),
            vm((NZ - 1, E, E), BF16),
            vm((E, E), BF16),
            vm((NZ - 1, E, E), BF16),
            vm((E, E), F32),
            vm((E, E), F32),
            vm((TB, TB), BF16),
            vm((TB, TB), BF16),
            vm((TB, TB), BF16),
            vm((TB, TB), BF16),
            vm((TB, E), F32),
            vm((TB, E), F32),
            vm((TB, E), F32),
            vm((TB, C), BF16),
            vm((TB, C), BF16),
            vm((C, TB), BF16),
            vm((C, TB), BF16),
            vm((NZ, 2, C, KB), BF16),
            vm((2, 4, 2, C, KB), BF16),
            vm((2, 4, 4, TB, DB), BF16),
            vm((4, 4, TB, DB), BF16),
            vm((3, 4, HALF, DB), BF16),
            vm((3, 4, HALF, DB), BF16),
            vm((4, HALF, DB), BF16),
            vm((4, HALF, DB), BF16),
            vm((3, HALF, DB), BF16),
            vm((3, HALF, DB), BF16),
            dma((2, 4, 2)), dma((2, 4, 2)),
            dma((6,)), dma((6,)),
            dma((6,)), dma((6,)),
            dma((8,)), dma((8,)),
            dma((7,)), dma((7,)),
            dma((7,)), dma((7,)),
            dma((2, 4, 2)), dma((2, 4, 2)),
            dma((4,)), dma((4,)),
            dma((6,)), dma((6,)),
            dma((6,)), dma((6,)),
        ],
        compiler_params=pltpu.CompilerParams(
            collective_id=0, has_side_effects=True, vmem_limit_bytes=56 * 1024 * 1024
        ),
        name="flipout_layer",
    )(tokens, in_mask, out_mask, w_mean.reshape(KB, C), w_sigma.reshape(KB, C), grad_out)
    attended, d_tokens, g_mean, g_sigma = pl.pallas_call(
        hand_over,
        out_shape=[jax.ShapeDtypeStruct(r.shape, r.dtype) for r in results],
        in_specs=[pl.BlockSpec(memory_space=pl.ANY)] * 4,
        out_specs=[pl.BlockSpec(memory_space=vm)] * 4,
        scratch_shapes=[dma((4,))],
        name="hand_over",
    )(*results)
    return attended, d_tokens, g_mean.reshape(KB, 1, C), g_sigma.reshape(KB, 1, C)


def solution(mesh):
    placed = (
        P("seq", "fsdp"),
        P("seq", "fsdp"),
        P("seq", "fsdp", None),
        P("seq", "fsdp", None),
        P("seq", "fsdp", None),
        P("seq", "fsdp"),
    )
    return jax.shard_map(
        local,
        mesh=mesh,
        in_specs=placed,
        out_specs=(P("seq", "fsdp"), P("seq", "fsdp"), P("seq", "fsdp", None), P("seq", "fsdp", None)),
        check_vma=False,
    )
```

```python
import jax
import jax.numpy as jnp
from jax import lax
from jax.experimental import pallas as pl
from jax.experimental.pallas import tpu as pltpu
from jax.sharding import PartitionSpec as P

EPSILON = 1e-06
MESH = pl.DeviceIdType.MESH
F32 = jnp.float32
BF16 = jnp.bfloat16
TB = 512
DB = 128
KB = 512
E = 128
C = 3 * E
NZ = 8
HALF = TB // 2


def nn(a, b):
    return lax.dot_general(a, b, (((1,), (0,)), ((), ())), preferred_element_type=F32)


def nt(a, b):
    return lax.dot_general(a, b, (((1,), (1,)), ((), ())), preferred_element_type=F32)


def kernel(
    tok, in_mask, out_mask, w_mean, w_sigma, gout,
    att_out, dtok_out, gm_out, gs_out,
    ta, sa, sgn, w_all, pm, ps, sts, str_, sus, sur, inc, suf, sc, sct, ds, dst, nu, dki, dvi,
    gb, gsb, gt, gst, gp, rr, bp, cr, xr, yr, xb, yb, xr2, yr2,
    zs, zr, ts, tr, ss, sr, cs, crs, st_s, st_r, su_s, su_r, rs_s, rs_r, eq_s, eq_r, bc_s, bc_r, bx_s, bx_r, by_s, by_r,
):
    s = lax.axis_index("seq")
    f = lax.axis_index("fsdp")
    c = lax.rem(f, 2)
    x = lax.rem(lax.div(f, 2), 4)
    y = lax.div(f, 8)
    oc = 1 - c

    def at_seq(k):
        return (lax.rem(s + k, NZ), f)

    def at_x(k):
        return (s, (y * 4 + lax.rem(x + k, 4)) * 2 + c)

    def at_y(k):
        return (s, (lax.rem(y + k, 4) * 4 + x) * 2 + c)

    partner = (s, (y * 4 + x) * 2 + oc)
    pending = []

    def copy(src, dst, send, recv, dev):
        return pltpu.make_async_remote_copy(
            src_ref=src, dst_ref=dst, send_sem=send, recv_sem=recv, device_id=dev, device_id_type=MESH
        )

    def start(src, dst, send, recv, dev):
        one = copy(src, dst, send, recv, dev)
        one.start()
        pending.append(one)

    def arrived(ref, send, recv):
        copy(ref, ref, send, recv, partner).wait_recv()

    barrier = pltpu.get_barrier_semaphore()
    peers = [at_seq(k) for k in range(1, NZ)] + [at_x(k) for k in (1, 2, 3)] + [at_y(k) for k in (1, 2, 3)] + [partner]
    for peer in peers:
        pl.semaphore_signal(barrier, inc=1, device_id=peer, device_id_type=MESH)

    ta[c, y, x] = tok[...]
    sa[c, y, x] = (2 * in_mask[...] - 1).astype(F32).astype(BF16)
    w_all[s, 0] = w_mean[...]
    w_all[s, 1] = w_sigma[...]
    pl.semaphore_wait(barrier, len(peers))

    def ring_out(way, hop, m):
        owner = lax.rem(s + (NZ - hop if way == 0 else hop), NZ)
        ref = w_all.at[owner, m]
        start(ref, ref, zs.at[way, hop, m], zr.at[way, hop, m], at_seq(1 if way == 0 else NZ - 1))

    def ring_in(way, hop, m):
        owner = lax.rem(s + (NZ - 1 - hop if way == 0 else 1 + hop), NZ)
        arrived(w_all.at[owner, m], zs.at[way, hop, m], zr.at[way, hop, m])

    def ring_step(hop, part):
        for way in (0, 1):
            m = part if way == 0 else 1 - part
            ring_in(way, hop, m)
            if hop < 2 or (hop == 2 and part == 0):
                ring_out(way, hop + 1, m)

    for part in (0, 1):
        ring_out(0, 0, part)
        ring_out(1, 0, 1 - part)

    for k in (1, 2, 3):
        start(ta.at[c, y, x], ta.at[c, y, x], ts.at[k - 1], tr.at[k - 1], at_x(k))
        start(sa.at[c, y, x], sa.at[c, y, x], ss.at[k - 1], sr.at[k - 1], at_y(k))
    for k in (1, 2, 3):
        arrived(ta.at[c, y, lax.rem(x + 4 - k, 4)], ts.at[k - 1], tr.at[k - 1])
    for k in (1, 2, 3):
        start(ta.at[c, y], ta.at[c, y], ts.at[2 + k], tr.at[2 + k], at_y(k))
    for k in (1, 2, 3):
        arrived(sa.at[c, lax.rem(y + 4 - k, 4), x], ss.at[k - 1], sr.at[k - 1])
    for k in (1, 2, 3):
        start(sa.at[c, :, x], sa.at[c, :, x], ss.at[2 + k], sr.at[2 + k], at_x(k))
    start(ta.at[c, y], ta.at[c, y], cs.at[0], crs.at[0], partner)
    start(sa.at[c, :, x], sa.at[c, :, x], cs.at[4], crs.at[4], partner)

    sgn[...] = (2 * out_mask[:, 0, :] - 1).astype(F32)
    ring_step(0, 0)
    ring_step(0, 1)
    ring_step(1, 0)
    for k in (1, 2, 3):
        yk = lax.rem(y + 4 - k, 4)
        arrived(ta.at[c, yk], ts.at[2 + k], tr.at[2 + k])
        start(ta.at[c, yk], ta.at[c, yk], cs.at[k], crs.at[k], partner)
        xk = lax.rem(x + 4 - k, 4)
        arrived(sa.at[c, :, xk], ss.at[2 + k], sr.at[2 + k])
        start(sa.at[c, :, xk], sa.at[c, :, xk], cs.at[4 + k], crs.at[4 + k], partner)
    ring_step(1, 1)
    for k in range(4):
        arrived(ta.at[oc, lax.rem(y + 4 - k, 4)], cs.at[k], crs.at[k])
        arrived(sa.at[oc, :, lax.rem(x + 4 - k, 4)], cs.at[4 + k], crs.at[4 + k])

    def columns(ref, e):
        row, first = lax.div(e, 2), 2 * lax.rem(e, 2)
        return jnp.concatenate([ref[j % 2, row, first + j // 2] for j in range(4)], axis=1)

    pm[...] = jnp.zeros_like(pm)
    ps[...] = jnp.zeros_like(ps)

    def project(first, stride, count):
        def one(i, carry):
            owner = lax.rem(s + first + i * stride, NZ)
            t = columns(ta, owner)
            pm[...] += nn(t, w_all[owner, 0])
            ps[...] += nn(t * columns(sa, owner), w_all[owner, 1])
            return carry

        lax.fori_loop(0, count, one, 0)

    project(NZ - 2, 1, 5)
    ring_step(2, 0)
    ring_step(2, 1)
    project(NZ - 3, 6, 2)
    ring_in(0, 3, 0)
    ring_in(1, 3, 1)
    project(4, 1, 1)

    so = sgn[...]
    pre = pm[...] + ps[...] * so
    uq, uk, v = pre[:, :E], pre[:, E : 2 * E], pre[:, 2 * E :]
    exp_q, exp_k = jnp.exp(jnp.minimum(uq, 0.0)), jnp.exp(jnp.minimum(uk, 0.0))
    q = jnp.where(uq > 0, uq + 1.0, exp_q)
    kf = jnp.where(uk > 0, uk + 1.0, exp_k)
    slope_q = jnp.where(uq > 0, 1.0, exp_q)
    slope_k = jnp.where(uk > 0, 1.0, exp_k)
    qb, kb, vb = q.astype(BF16), kf.astype(BF16), v.astype(BF16)

    sts[...] = nn(jnp.transpose(kf).astype(BF16), vb).astype(BF16)
    for k in range(1, NZ):
        @pl.when(s + k < NZ)
        def _():
            copy(sts, str_.at[k - 1], st_s.at[k - 1], st_r.at[k - 1], at_seq(k)).start()

    rows = lax.broadcasted_iota(jnp.int32, (TB, TB), 0)
    cols = lax.broadcasted_iota(jnp.int32, (TB, TB), 1)
    sc[...] = jnp.where(rows >= cols, nt(qb, kb), 0.0).astype(BF16)
    sct[...] = jnp.where(rows <= cols, nt(kb, qb), 0.0).astype(BF16)
    nu[...] = nn(sc[...], vb)
    inc[...] = jnp.zeros_like(inc)
    for k in range(1, NZ):
        @pl.when(s >= k)
        def _():
            arrived(str_.at[k - 1], st_s.at[k - 1], st_r.at[k - 1])
            inc[...] += str_[k - 1].astype(F32)

    inb = inc[...].astype(BF16)
    num = nu[...] + nn(qb, inb)
    inv = lax.rsqrt(jnp.mean(num * num, axis=-1, keepdims=True) + EPSILON)
    normed = num * inv
    att_out[...] = normed.astype(BF16)
    up = gout[...].astype(F32)
    dn = inv * (up - normed * jnp.mean(up * normed, axis=-1, keepdims=True))
    dnb = dn.astype(BF16)
    sus[...] = nn(jnp.transpose(q).astype(BF16), dnb).astype(BF16)
    for k in range(1, NZ):
        @pl.when(s >= k)
        def _():
            copy(sus, sur.at[k - 1], su_s.at[k - 1], su_r.at[k - 1], at_seq(NZ - k)).start()

    every, query, rest = pl.ds(0, C), pl.ds(0, E), pl.ds(E, C - E)

    def partials(first, stride, count, part):
        def one(i, carry):
            e = lax.rem(s + first + i * stride, NZ)
            t = columns(ta, e)
            gp[e, 0, part] = nn(gt[part, :], t).astype(BF16)
            gp[e, 1, part] = nn(gst[part, :], t * columns(sa, e)).astype(BF16)
            return carry

        lax.fori_loop(0, count, one, 0)

    def in_two(way, left, m):
        return left == 4 or (left == 3 and m != way)

    def send_sum(way, left, m, part, send, recv):
        e = lax.rem(s + (left if way == 0 else NZ - left), NZ)
        start(gp.at[e, m, part], rr.at[way, left - 1, m, part], send, recv, at_seq(1 if way == 0 else NZ - 1))

    def query_out(way, left, m):
        send_sum(way, left, m, query, eq_s.at[way, left - 3], eq_r.at[way, left - 3])

    def sum_out(way, left, m):
        e = lax.rem(s + (left if way == 0 else NZ - left), NZ)
        part = rest if in_two(way, left, m) else every
        if part is every:
            if in_two(way, left + 1, m):
                arrived(rr.at[way, left, m, query], eq_s.at[way, left - 2], eq_r.at[way, left - 2])
                arrived(rr.at[way, left, m, rest], rs_s.at[way, left, m], rs_r.at[way, left, m])
            else:
                arrived(rr.at[way, left, m], rs_s.at[way, left, m], rs_r.at[way, left, m])
            gp[e, m] = (gp[e, m].astype(F32) + rr[way, left, m].astype(F32)).astype(BF16)
        send_sum(way, left, m, part, rs_s.at[way, left - 1, m], rs_r.at[way, left - 1, m])

    ds[...] = jnp.where(rows >= cols, nt(dnb, vb), 0.0).astype(BF16)
    dq = (nn(ds[...], kb) + nt(dnb, inb)) * slope_q
    gt[query, :] = jnp.transpose(dq).astype(BF16)
    gst[query, :] = jnp.transpose(dq * so[:, :E]).astype(BF16)
    partials(4, 1, 1, query)
    query_out(0, 4, 0)
    query_out(1, 4, 1)
    partials(3, 2, 2, query)
    query_out(0, 3, 1)
    query_out(1, 3, 0)
    dst[...] = jnp.where(rows <= cols, nt(vb, dnb), 0.0).astype(BF16)
    dki[...] = nn(dst[...], qb)
    dvi[...] = nn(sct[...], dnb)
    suf[...] = jnp.zeros_like(suf)
    for k in range(1, NZ):
        @pl.when(s + k < NZ)
        def _():
            arrived(sur.at[k - 1], su_s.at[k - 1], su_r.at[k - 1])
            suf[...] += sur[k - 1].astype(F32)

    sfb = suf[...].astype(BF16)
    dk = (dki[...] + nt(vb, sfb)) * slope_k
    dv = dvi[...] + nn(kb, sfb)
    later = jnp.concatenate([dk, dv], axis=1)
    gt[rest, :] = jnp.transpose(later).astype(BF16)
    gst[rest, :] = jnp.transpose(later * so[:, E:]).astype(BF16)

    partials(4, 1, 1, rest)
    sum_out(0, 4, 0)
    sum_out(1, 4, 1)
    partials(3, 2, 2, rest)
    sum_out(0, 3, 1)
    sum_out(1, 3, 0)

    gb[:, :E] = dq.astype(BF16)
    gb[:, E:] = later.astype(BF16)
    gsb[:, :E] = (dq * so[:, :E]).astype(BF16)
    gsb[:, E:] = (later * so[:, E:]).astype(BF16)

    def back(e, carry):
        term = nt(gb[...], w_all[e, 0]) + columns(sa, e).astype(F32) * nt(gsb[...], w_all[e, 1])
        term = term.astype(BF16)
        row, first = lax.div(e, 2), 2 * lax.rem(e, 2)
        for j in range(4):
            bp[j % 2, row, first + j // 2] = term[:, j * DB : (j + 1) * DB]
        return carry

    for g in range(4):
        lax.fori_loop(2 * g, 2 * g + 2, back, 0)
        start(bp.at[oc, g], cr.at[g], bc_s.at[g], bc_r.at[g], partner)

    sum_out(0, 3, 0)
    sum_out(1, 3, 1)
    partials(NZ - 2, 1, 5, every)

    for g in range(4):
        arrived(cr.at[g], bc_s.at[g], bc_r.at[g])

    def join(i, carry):
        a, b = lax.div(i, 4), lax.rem(i, 4)
        bp[c, a, b] = (bp[c, a, b].astype(F32) + cr[a, b].astype(F32)).astype(BF16)
        return carry

    lax.fori_loop(0, 16, join, 0)
    top, low = pl.ds(0, HALF), pl.ds(HALF, HALF)
    for k in (1, 2, 3):
        start(bp.at[c, :, lax.rem(x + k, 4), top], xr.at[k - 1], bx_s.at[k - 1], bx_r.at[k - 1], at_x(k))
        start(bp.at[c, lax.rem(y + k, 4), :, low], yr.at[k - 1], by_s.at[k - 1], by_r.at[k - 1], at_y(k))

    sum_out(0, 2, 1)
    sum_out(1, 2, 0)
    sum_out(0, 2, 0)
    sum_out(1, 2, 1)

    for k in (1, 2, 3):
        arrived(xr.at[k - 1], bx_s.at[k - 1], bx_r.at[k - 1])
        arrived(yr.at[k - 1], by_s.at[k - 1], by_r.at[k - 1])
    for i in range(4):
        total = bp[c, i, x, top].astype(F32)
        other = bp[c, y, i, low].astype(F32)
        for k in range(3):
            total += xr[k, i].astype(F32)
            other += yr[k, i].astype(F32)
        xb[i] = total.astype(BF16)
        yb[i] = other.astype(BF16)
    for k in (1, 2, 3):
        start(xb.at[lax.rem(y + k, 4)], xr2.at[k - 1], by_s.at[2 + k], by_r.at[2 + k], at_y(k))
        start(yb.at[lax.rem(x + k, 4)], yr2.at[k - 1], bx_s.at[2 + k], bx_r.at[2 + k], at_x(k))

    sum_out(0, 1, 1)
    sum_out(1, 1, 0)

    for k in (1, 2, 3):
        arrived(xr2.at[k - 1], by_s.at[2 + k], by_r.at[2 + k])
        arrived(yr2.at[k - 1], bx_s.at[2 + k], bx_r.at[2 + k])
    total = xb[y].astype(F32)
    other = yb[x].astype(F32)
    for k in range(3):
        total += xr2[k].astype(F32)
        other += yr2[k].astype(F32)
    dtok_out[top, :] = total.astype(BF16)
    dtok_out[low, :] = other.astype(BF16)

    sum_out(0, 1, 0)
    sum_out(1, 1, 1)
    for m, out in ((1, gs_out), (0, gm_out)):
        for way in (0, 1):
            arrived(rr.at[way, 0, m], rs_s.at[way, 0, m], rs_r.at[way, 0, m])
        total = gp[s, m].astype(F32) + rr[0, 0, m].astype(F32) + rr[1, 0, m].astype(F32)
        out[...] = jnp.transpose(total).astype(BF16)

    for one in pending:
        one.wait_send()
    for k in range(1, NZ):
        @pl.when(s + k < NZ)
        def _():
            copy(sts, str_.at[k - 1], st_s.at[k - 1], st_r.at[k - 1], at_seq(k)).wait_send()

        @pl.when(s >= k)
        def _():
            copy(sus, sur.at[k - 1], su_s.at[k - 1], su_r.at[k - 1], at_seq(NZ - k)).wait_send()


def hand_over(*refs):
    n = len(refs) // 2
    copies = [pltpu.make_async_copy(refs[i], refs[n + i], refs[2 * n].at[i]) for i in range(n)]
    for one in copies:
        one.start()
    for one in copies:
        one.wait()


def local(tokens, in_mask, out_mask, w_mean, w_sigma, grad_out):
    vm = pltpu.VMEM
    dma = pltpu.SemaphoreType.DMA
    results = pl.pallas_call(
        kernel,
        out_shape=(
            jax.ShapeDtypeStruct((TB, E), BF16),
            jax.ShapeDtypeStruct((TB, DB), BF16),
            jax.ShapeDtypeStruct((KB, C), BF16),
            jax.ShapeDtypeStruct((KB, C), BF16),
        ),
        in_specs=[pl.BlockSpec(memory_space=vm)] * 6,
        out_specs=[pl.BlockSpec(memory_space=vm)] * 4,
        scratch_shapes=[
            vm((2, 4, 4, TB, DB), BF16),
            vm((2, 4, 4, TB, DB), BF16),
            vm((TB, C), F32),
            vm((NZ, 2, KB, C), BF16),
            vm((TB, C), F32),
            vm((TB, C), F32),
            vm((E, E), BF16),
            vm((NZ - 1, E, E), BF16),
            vm((E, E), BF16),
            vm((NZ - 1, E, E), BF16),
            vm((E, E), F32),
            vm((E, E), F32),
            vm((TB, TB), BF16),
            vm((TB, TB), BF16),
            vm((TB, TB), BF16),
            vm((TB, TB), BF16),
            vm((TB, E), F32),
            vm((TB, E), F32),
            vm((TB, E), F32),
            vm((TB, C), BF16),
            vm((TB, C), BF16),
            vm((C, TB), BF16),
            vm((C, TB), BF16),
            vm((NZ, 2, C, KB), BF16),
            vm((2, 4, 2, C, KB), BF16),
            vm((2, 4, 4, TB, DB), BF16),
            vm((4, 4, TB, DB), BF16),
            vm((3, 4, HALF, DB), BF16),
            vm((3, 4, HALF, DB), BF16),
            vm((4, HALF, DB), BF16),
            vm((4, HALF, DB), BF16),
            vm((3, HALF, DB), BF16),
            vm((3, HALF, DB), BF16),
            dma((2, 4, 2)), dma((2, 4, 2)),
            dma((6,)), dma((6,)),
            dma((6,)), dma((6,)),
            dma((8,)), dma((8,)),
            dma((7,)), dma((7,)),
            dma((7,)), dma((7,)),
            dma((2, 4, 2)), dma((2, 4, 2)),
            dma((2, 2)), dma((2, 2)),
            dma((4,)), dma((4,)),
            dma((6,)), dma((6,)),
            dma((6,)), dma((6,)),
        ],
        compiler_params=pltpu.CompilerParams(
            collective_id=0, has_side_effects=True, vmem_limit_bytes=56 * 1024 * 1024
        ),
        name="flipout_layer",
    )(tokens, in_mask, out_mask, w_mean.reshape(KB, C), w_sigma.reshape(KB, C), grad_out)
    attended, d_tokens, g_mean, g_sigma = pl.pallas_call(
        hand_over,
        out_shape=[jax.ShapeDtypeStruct(r.shape, r.dtype) for r in results],
        in_specs=[pl.BlockSpec(memory_space=pl.ANY)] * 4,
        out_specs=[pl.BlockSpec(memory_space=vm)] * 4,
        scratch_shapes=[dma((4,))],
        name="hand_over",
    )(*results)
    return attended, d_tokens, g_mean.reshape(KB, 1, C), g_sigma.reshape(KB, 1, C)


def solution(mesh):
    placed = (
        P("seq", "fsdp"),
        P("seq", "fsdp"),
        P("seq", "fsdp", None),
        P("seq", "fsdp", None),
        P("seq", "fsdp", None),
        P("seq", "fsdp"),
    )
    return jax.shard_map(
        local,
        mesh=mesh,
        in_specs=placed,
        out_specs=(P("seq", "fsdp"), P("seq", "fsdp"), P("seq", "fsdp", None), P("seq", "fsdp", None)),
        check_vma=False,
    )
```

```python
import jax
import jax.numpy as jnp
from jax import lax
from jax.experimental import pallas as pl
from jax.experimental.pallas import tpu as pltpu
from jax.sharding import PartitionSpec as P

EPSILON = 1e-06
MESH = pl.DeviceIdType.MESH
F32 = jnp.float32
BF16 = jnp.bfloat16
TB = 512
DB = 128
KB = 512
E = 128
C = 3 * E
NZ = 8
HALF = TB // 2


def nn(a, b):
    return lax.dot_general(a, b, (((1,), (0,)), ((), ())), preferred_element_type=F32)


def nt(a, b):
    return lax.dot_general(a, b, (((1,), (1,)), ((), ())), preferred_element_type=F32)


def kernel(
    tok, in_mask, out_mask, w_mean, w_sigma, gout,
    att_out, dtok_out, gm_out, gs_out,
    ta, sa, sgn, w_all, pm, ps, sts, str_, sus, sur, inc, suf, sc, sct, ds, dst, nu, dki, dvi,
    gb, gsb, gt, gst, gp, rr, bp, cr, xr, yr, xb, yb, xr2, yr2,
    zs, zr, ts, tr, ss, sr, cs, crs, st_s, st_r, su_s, su_r, rs_s, rs_r, eq_s, eq_r, bc_s, bc_r, bx_s, bx_r, by_s, by_r,
):
    s = lax.axis_index("seq")
    f = lax.axis_index("fsdp")
    c = lax.rem(f, 2)
    x = lax.rem(lax.div(f, 2), 4)
    y = lax.div(f, 8)
    oc = 1 - c

    def at_seq(k):
        return (lax.rem(s + k, NZ), f)

    def at_x(k):
        return (s, (y * 4 + lax.rem(x + k, 4)) * 2 + c)

    def at_y(k):
        return (s, (lax.rem(y + k, 4) * 4 + x) * 2 + c)

    partner = (s, (y * 4 + x) * 2 + oc)
    pending = []

    def copy(src, dst, send, recv, dev):
        return pltpu.make_async_remote_copy(
            src_ref=src, dst_ref=dst, send_sem=send, recv_sem=recv, device_id=dev, device_id_type=MESH
        )

    def start(src, dst, send, recv, dev):
        one = copy(src, dst, send, recv, dev)
        one.start()
        pending.append(one)

    def arrived(ref, send, recv):
        copy(ref, ref, send, recv, partner).wait_recv()

    barrier = pltpu.get_barrier_semaphore()
    peers = [at_seq(k) for k in range(1, NZ)] + [at_x(k) for k in (1, 2, 3)] + [at_y(k) for k in (1, 2, 3)] + [partner]
    for peer in peers:
        pl.semaphore_signal(barrier, inc=1, device_id=peer, device_id_type=MESH)

    ta[c, y, x] = tok[...]
    sa[c, y, x] = (2 * in_mask[...] - 1).astype(F32).astype(BF16)
    w_all[s, 0] = w_mean[...]
    w_all[s, 1] = w_sigma[...]
    pl.semaphore_wait(barrier, len(peers))

    def ring_out(way, hop, m):
        owner = lax.rem(s + (NZ - hop if way == 0 else hop), NZ)
        ref = w_all.at[owner, m]
        start(ref, ref, zs.at[way, hop, m], zr.at[way, hop, m], at_seq(1 if way == 0 else NZ - 1))

    def ring_in(way, hop, m):
        owner = lax.rem(s + (NZ - 1 - hop if way == 0 else 1 + hop), NZ)
        arrived(w_all.at[owner, m], zs.at[way, hop, m], zr.at[way, hop, m])

    def ring_step(hop, part):
        for way in (0, 1):
            m = part if way == 0 else 1 - part
            ring_in(way, hop, m)
            if hop < 2 or (hop == 2 and part == 0):
                ring_out(way, hop + 1, m)

    for part in (0, 1):
        ring_out(0, 0, part)
        ring_out(1, 0, 1 - part)

    for k in (1, 2, 3):
        start(ta.at[c, y, x], ta.at[c, y, x], ts.at[k - 1], tr.at[k - 1], at_x(k))
        start(sa.at[c, y, x], sa.at[c, y, x], ss.at[k - 1], sr.at[k - 1], at_y(k))
    for k in (1, 2, 3):
        arrived(ta.at[c, y, lax.rem(x + 4 - k, 4)], ts.at[k - 1], tr.at[k - 1])
    for k in (1, 2, 3):
        start(ta.at[c, y], ta.at[c, y], ts.at[2 + k], tr.at[2 + k], at_y(k))
    for k in (1, 2, 3):
        arrived(sa.at[c, lax.rem(y + 4 - k, 4), x], ss.at[k - 1], sr.at[k - 1])
    for k in (1, 2, 3):
        start(sa.at[c, :, x], sa.at[c, :, x], ss.at[2 + k], sr.at[2 + k], at_x(k))
    start(ta.at[c, y], ta.at[c, y], cs.at[0], crs.at[0], partner)
    start(sa.at[c, :, x], sa.at[c, :, x], cs.at[4], crs.at[4], partner)

    sgn[...] = (2 * out_mask[:, 0, :] - 1).astype(F32)
    ring_step(0, 0)
    ring_step(0, 1)
    ring_step(1, 0)
    for k in (1, 2, 3):
        yk = lax.rem(y + 4 - k, 4)
        arrived(ta.at[c, yk], ts.at[2 + k], tr.at[2 + k])
        start(ta.at[c, yk], ta.at[c, yk], cs.at[k], crs.at[k], partner)
        xk = lax.rem(x + 4 - k, 4)
        arrived(sa.at[c, :, xk], ss.at[2 + k], sr.at[2 + k])
        start(sa.at[c, :, xk], sa.at[c, :, xk], cs.at[4 + k], crs.at[4 + k], partner)
    ring_step(1, 1)
    for k in range(4):
        arrived(ta.at[oc, lax.rem(y + 4 - k, 4)], cs.at[k], crs.at[k])
        arrived(sa.at[oc, :, lax.rem(x + 4 - k, 4)], cs.at[4 + k], crs.at[4 + k])

    def columns(ref, e):
        row, first = lax.div(e, 2), 2 * lax.rem(e, 2)
        return jnp.concatenate([ref[j % 2, row, first + j // 2] for j in range(4)], axis=1)

    pm[...] = jnp.zeros_like(pm)
    ps[...] = jnp.zeros_like(ps)

    def project(first, stride, count):
        def one(i, carry):
            owner = lax.rem(s + first + i * stride, NZ)
            t = columns(ta, owner)
            pm[...] += nn(t, w_all[owner, 0])
            ps[...] += nn(t * columns(sa, owner), w_all[owner, 1])
            return carry

        lax.fori_loop(0, count, one, 0)

    project(NZ - 2, 1, 5)
    ring_step(2, 0)
    ring_step(2, 1)
    project(NZ - 3, 6, 2)
    ring_in(0, 3, 0)
    ring_in(1, 3, 1)
    project(4, 1, 1)

    so = sgn[...]
    pre = pm[...] + ps[...] * so
    uq, uk, v = pre[:, :E], pre[:, E : 2 * E], pre[:, 2 * E :]
    exp_q, exp_k = jnp.exp(jnp.minimum(uq, 0.0)), jnp.exp(jnp.minimum(uk, 0.0))
    q = jnp.where(uq > 0, uq + 1.0, exp_q)
    kf = jnp.where(uk > 0, uk + 1.0, exp_k)
    slope_q = jnp.where(uq > 0, 1.0, exp_q)
    slope_k = jnp.where(uk > 0, 1.0, exp_k)
    qb, kb, vb = q.astype(BF16), kf.astype(BF16), v.astype(BF16)

    sts[...] = nn(jnp.transpose(kf).astype(BF16), vb).astype(BF16)
    for k in range(1, NZ):
        @pl.when(s + k < NZ)
        def _():
            copy(sts, str_.at[k - 1], st_s.at[k - 1], st_r.at[k - 1], at_seq(k)).start()

    rows = lax.broadcasted_iota(jnp.int32, (TB, TB), 0)
    cols = lax.broadcasted_iota(jnp.int32, (TB, TB), 1)
    sc[...] = jnp.where(rows >= cols, nt(qb, kb), 0.0).astype(BF16)
    sct[...] = jnp.where(rows <= cols, nt(kb, qb), 0.0).astype(BF16)
    nu[...] = nn(sc[...], vb)
    qt = jnp.transpose(q).astype(BF16)
    up = gout[...].astype(F32)
    inc[...] = jnp.zeros_like(inc)
    for k in range(1, NZ):
        @pl.when(s >= k)
        def _():
            arrived(str_.at[k - 1], st_s.at[k - 1], st_r.at[k - 1])
            inc[...] += str_[k - 1].astype(F32)

    inb = inc[...].astype(BF16)
    num = nu[...] + nn(qb, inb)
    inv = lax.rsqrt(jnp.mean(num * num, axis=-1, keepdims=True) + EPSILON)
    normed = num * inv
    dn = inv * (up - normed * jnp.mean(up * normed, axis=-1, keepdims=True))
    dnb = dn.astype(BF16)
    sus[...] = nn(qt, dnb).astype(BF16)
    for k in range(1, NZ):
        @pl.when(s >= k)
        def _():
            copy(sus, sur.at[k - 1], su_s.at[k - 1], su_r.at[k - 1], at_seq(NZ - k)).start()

    every, query, rest = pl.ds(0, C), pl.ds(0, E), pl.ds(E, C - E)

    def partials(first, stride, count, part):
        def one(i, carry):
            e = lax.rem(s + first + i * stride, NZ)
            t = columns(ta, e)
            gp[e, 0, part] = nn(gt[part, :], t).astype(BF16)
            gp[e, 1, part] = nn(gst[part, :], t * columns(sa, e)).astype(BF16)
            return carry

        lax.fori_loop(0, count, one, 0)

    def in_two(way, left, m):
        return left == 4 or (left == 3 and m != way)

    def send_sum(way, left, m, part, send, recv):
        e = lax.rem(s + (left if way == 0 else NZ - left), NZ)
        start(gp.at[e, m, part], rr.at[way, left - 1, m, part], send, recv, at_seq(1 if way == 0 else NZ - 1))

    def query_out(way, left, m):
        send_sum(way, left, m, query, eq_s.at[way, left - 3], eq_r.at[way, left - 3])

    def sum_out(way, left, m):
        e = lax.rem(s + (left if way == 0 else NZ - left), NZ)
        part = rest if in_two(way, left, m) else every
        if part is every:
            if in_two(way, left + 1, m):
                arrived(rr.at[way, left, m, query], eq_s.at[way, left - 2], eq_r.at[way, left - 2])
                arrived(rr.at[way, left, m, rest], rs_s.at[way, left, m], rs_r.at[way, left, m])
            else:
                arrived(rr.at[way, left, m], rs_s.at[way, left, m], rs_r.at[way, left, m])
            gp[e, m] = (gp[e, m].astype(F32) + rr[way, left, m].astype(F32)).astype(BF16)
        send_sum(way, left, m, part, rs_s.at[way, left - 1, m], rs_r.at[way, left - 1, m])

    att_out[...] = normed.astype(BF16)
    ds[...] = jnp.where(rows >= cols, nt(dnb, vb), 0.0).astype(BF16)
    dq = (nn(ds[...], kb) + nt(dnb, inb)) * slope_q
    gt[query, :] = jnp.transpose(dq).astype(BF16)
    gst[query, :] = jnp.transpose(dq * so[:, :E]).astype(BF16)
    partials(4, 1, 1, query)
    query_out(0, 4, 0)
    query_out(1, 4, 1)
    partials(3, 2, 2, query)
    query_out(0, 3, 1)
    query_out(1, 3, 0)
    dst[...] = jnp.where(rows <= cols, nt(vb, dnb), 0.0).astype(BF16)
    dki[...] = nn(dst[...], qb)
    dvi[...] = nn(sct[...], dnb)
    suf[...] = jnp.zeros_like(suf)
    for k in range(1, NZ):
        @pl.when(s + k < NZ)
        def _():
            arrived(sur.at[k - 1], su_s.at[k - 1], su_r.at[k - 1])
            suf[...] += sur[k - 1].astype(F32)

    sfb = suf[...].astype(BF16)
    dk = (dki[...] + nt(vb, sfb)) * slope_k
    dv = dvi[...] + nn(kb, sfb)
    later = jnp.concatenate([dk, dv], axis=1)
    gt[rest, :] = jnp.transpose(later).astype(BF16)
    gst[rest, :] = jnp.transpose(later * so[:, E:]).astype(BF16)

    partials(4, 1, 1, rest)
    sum_out(0, 4, 0)
    sum_out(1, 4, 1)
    partials(3, 2, 2, rest)
    sum_out(0, 3, 1)
    sum_out(1, 3, 0)

    gb[:, :E] = dq.astype(BF16)
    gb[:, E:] = later.astype(BF16)
    gsb[:, :E] = (dq * so[:, :E]).astype(BF16)
    gsb[:, E:] = (later * so[:, E:]).astype(BF16)

    def back(e, carry):
        term = nt(gb[...], w_all[e, 0]) + columns(sa, e).astype(F32) * nt(gsb[...], w_all[e, 1])
        term = term.astype(BF16)
        row, first = lax.div(e, 2), 2 * lax.rem(e, 2)
        for j in range(4):
            bp[j % 2, row, first + j // 2] = term[:, j * DB : (j + 1) * DB]
        return carry

    for g in range(4):
        lax.fori_loop(2 * g, 2 * g + 2, back, 0)
        start(bp.at[oc, g], cr.at[g], bc_s.at[g], bc_r.at[g], partner)

    sum_out(0, 3, 0)
    sum_out(1, 3, 1)
    partials(NZ - 2, 1, 5, every)

    for g in range(4):
        arrived(cr.at[g], bc_s.at[g], bc_r.at[g])

    def join(i, carry):
        a, b = lax.div(i, 4), lax.rem(i, 4)
        bp[c, a, b] = (bp[c, a, b].astype(F32) + cr[a, b].astype(F32)).astype(BF16)
        return carry

    lax.fori_loop(0, 16, join, 0)
    top, low = pl.ds(0, HALF), pl.ds(HALF, HALF)
    for k in (1, 2, 3):
        start(bp.at[c, :, lax.rem(x + k, 4), top], xr.at[k - 1], bx_s.at[k - 1], bx_r.at[k - 1], at_x(k))
        start(bp.at[c, lax.rem(y + k, 4), :, low], yr.at[k - 1], by_s.at[k - 1], by_r.at[k - 1], at_y(k))

    sum_out(0, 2, 1)
    sum_out(1, 2, 0)
    sum_out(0, 2, 0)
    sum_out(1, 2, 1)

    for k in (1, 2, 3):
        arrived(xr.at[k - 1], bx_s.at[k - 1], bx_r.at[k - 1])
        arrived(yr.at[k - 1], by_s.at[k - 1], by_r.at[k - 1])
    for i in range(4):
        total = bp[c, i, x, top].astype(F32)
        other = bp[c, y, i, low].astype(F32)
        for k in range(3):
            total += xr[k, i].astype(F32)
            other += yr[k, i].astype(F32)
        xb[i] = total.astype(BF16)
        yb[i] = other.astype(BF16)
    for k in (1, 2, 3):
        start(xb.at[lax.rem(y + k, 4)], xr2.at[k - 1], by_s.at[2 + k], by_r.at[2 + k], at_y(k))
        start(yb.at[lax.rem(x + k, 4)], yr2.at[k - 1], bx_s.at[2 + k], bx_r.at[2 + k], at_x(k))

    sum_out(0, 1, 1)
    sum_out(1, 1, 0)

    for k in (1, 2, 3):
        arrived(xr2.at[k - 1], by_s.at[2 + k], by_r.at[2 + k])
        arrived(yr2.at[k - 1], bx_s.at[2 + k], bx_r.at[2 + k])
    total = xb[y].astype(F32)
    other = yb[x].astype(F32)
    for k in range(3):
        total += xr2[k].astype(F32)
        other += yr2[k].astype(F32)
    dtok_out[top, :] = total.astype(BF16)
    dtok_out[low, :] = other.astype(BF16)

    sum_out(0, 1, 0)
    sum_out(1, 1, 1)
    for m, out in ((1, gs_out), (0, gm_out)):
        for way in (0, 1):
            arrived(rr.at[way, 0, m], rs_s.at[way, 0, m], rs_r.at[way, 0, m])
        total = gp[s, m].astype(F32) + rr[0, 0, m].astype(F32) + rr[1, 0, m].astype(F32)
        out[...] = jnp.transpose(total).astype(BF16)

    for one in pending:
        one.wait_send()
    for k in range(1, NZ):
        @pl.when(s + k < NZ)
        def _():
            copy(sts, str_.at[k - 1], st_s.at[k - 1], st_r.at[k - 1], at_seq(k)).wait_send()

        @pl.when(s >= k)
        def _():
            copy(sus, sur.at[k - 1], su_s.at[k - 1], su_r.at[k - 1], at_seq(NZ - k)).wait_send()


def hand_over(*refs):
    n = len(refs) // 2
    copies = [pltpu.make_async_copy(refs[i], refs[n + i], refs[2 * n].at[i]) for i in range(n)]
    for one in copies:
        one.start()
    for one in copies:
        one.wait()


def local(tokens, in_mask, out_mask, w_mean, w_sigma, grad_out):
    vm = pltpu.VMEM
    dma = pltpu.SemaphoreType.DMA
    results = pl.pallas_call(
        kernel,
        out_shape=(
            jax.ShapeDtypeStruct((TB, E), BF16),
            jax.ShapeDtypeStruct((TB, DB), BF16),
            jax.ShapeDtypeStruct((KB, C), BF16),
            jax.ShapeDtypeStruct((KB, C), BF16),
        ),
        in_specs=[pl.BlockSpec(memory_space=vm)] * 6,
        out_specs=[pl.BlockSpec(memory_space=vm)] * 4,
        scratch_shapes=[
            vm((2, 4, 4, TB, DB), BF16),
            vm((2, 4, 4, TB, DB), BF16),
            vm((TB, C), F32),
            vm((NZ, 2, KB, C), BF16),
            vm((TB, C), F32),
            vm((TB, C), F32),
            vm((E, E), BF16),
            vm((NZ - 1, E, E), BF16),
            vm((E, E), BF16),
            vm((NZ - 1, E, E), BF16),
            vm((E, E), F32),
            vm((E, E), F32),
            vm((TB, TB), BF16),
            vm((TB, TB), BF16),
            vm((TB, TB), BF16),
            vm((TB, TB), BF16),
            vm((TB, E), F32),
            vm((TB, E), F32),
            vm((TB, E), F32),
            vm((TB, C), BF16),
            vm((TB, C), BF16),
            vm((C, TB), BF16),
            vm((C, TB), BF16),
            vm((NZ, 2, C, KB), BF16),
            vm((2, 4, 2, C, KB), BF16),
            vm((2, 4, 4, TB, DB), BF16),
            vm((4, 4, TB, DB), BF16),
            vm((3, 4, HALF, DB), BF16),
            vm((3, 4, HALF, DB), BF16),
            vm((4, HALF, DB), BF16),
            vm((4, HALF, DB), BF16),
            vm((3, HALF, DB), BF16),
            vm((3, HALF, DB), BF16),
            dma((2, 4, 2)), dma((2, 4, 2)),
            dma((6,)), dma((6,)),
            dma((6,)), dma((6,)),
            dma((8,)), dma((8,)),
            dma((7,)), dma((7,)),
            dma((7,)), dma((7,)),
            dma((2, 4, 2)), dma((2, 4, 2)),
            dma((2, 2)), dma((2, 2)),
            dma((4,)), dma((4,)),
            dma((6,)), dma((6,)),
            dma((6,)), dma((6,)),
        ],
        compiler_params=pltpu.CompilerParams(
            collective_id=0, has_side_effects=True, vmem_limit_bytes=56 * 1024 * 1024
        ),
        name="flipout_layer",
    )(tokens, in_mask, out_mask, w_mean.reshape(KB, C), w_sigma.reshape(KB, C), grad_out)
    attended, d_tokens, g_mean, g_sigma = pl.pallas_call(
        hand_over,
        out_shape=[jax.ShapeDtypeStruct(r.shape, r.dtype) for r in results],
        in_specs=[pl.BlockSpec(memory_space=pl.ANY)] * 4,
        out_specs=[pl.BlockSpec(memory_space=vm)] * 4,
        scratch_shapes=[dma((4,))],
        name="hand_over",
    )(*results)
    return attended, d_tokens, g_mean.reshape(KB, 1, C), g_sigma.reshape(KB, 1, C)


def solution(mesh):
    placed = (
        P("seq", "fsdp"),
        P("seq", "fsdp"),
        P("seq", "fsdp", None),
        P("seq", "fsdp", None),
        P("seq", "fsdp", None),
        P("seq", "fsdp"),
    )
    return jax.shard_map(
        local,
        mesh=mesh,
        in_specs=placed,
        out_specs=(P("seq", "fsdp"), P("seq", "fsdp"), P("seq", "fsdp", None), P("seq", "fsdp", None)),
        check_vma=False,
    )
```
